128 devices in a mesh: gx: 8 (over x, core), gy: 4 (over y), gz: 4 (over z).
Axes of the slice: x: 4, y: 4, z: 4, core: 2. Of those that a mesh axis runs over, the one named last changes fastest.
Arguments:
- rhs: float32 [8, 4, 4, 1024, 128], P('gx', 'gy', 'gz'), may hold values from -40 to 40
- diagonal: float32 [8, 4, 4, 1024], P('gx', 'gy', 'gz'), may hold values from 0.05 to 1
- couple: float32 [8, 4, 4, 6, 1024], P('gx', 'gy', 'gz'), may hold values from 0 to 1
- neighbours: int32 [8, 4, 4, 6, 1024], P('gx', 'gy', 'gz'), may hold values from 0 to 2559
- export_rows: int32 [8, 4, 4, 6, 256], P('gx', 'gy', 'gz'), may hold values from 0 to 1023
- local_inverse: float32 [8, 4, 4, 1024, 2560], P('gx', 'gy', 'gz'), may hold values from -1 to 1
- basis: float32 [8, 4, 4, 64, 1024], P('gx', 'gy', 'gz'), may hold values from -0.1875 to 0.1875
- coarse_inverse: float32 [8192, 8192], P(('gx', 'gy', 'gz')), may hold values from -1 to 1
- owner: int32 [128], replicated, may hold values from 0 to 127, each once
Outputs:
- solution: float32 [8, 4, 4, 1024, 128], P('gx', 'gy', 'gz')
- residual: float32 [8, 4, 4, 1024, 128], P('gx', 'gy', 'gz')
The draws below stay inside these ranges and needn't reach their ends.
Inputs may be any that keep to these rules, and one draw needn't show every extreme that they name: `owner`: each coarse block belongs to exactly one subdomain.
All inputs are finite; a program needn't handle non-finite values.
Results may differ from the reference program's by a relative error of at most 0.0001.
Values sent between devices are 32-bit elements; how exact they have to be, the bound alone decides.
A program may use at most 128 MiB of HBM per device.

```python
import math
import jax
import jax.numpy as jnp
from jax import lax

OWN = 1024
NRHS = 128
K = 64
ITERS = 2
OVR = 256
NEXT = 2560
DK = 8192
N_GX = 8
N_GY = 4
N_GZ = 4
DEVICES = 128


def draw_local_inverse(key, part):
    key = jax.random.fold_in(key, 11)
    shape = (N_GX, N_GY, N_GZ, OWN, NEXT)
    noise = jnp.clip(jax.random.normal(key, shape, jnp.float32), -4.0, 4.0)
    rows = lax.broadcasted_iota(jnp.int32, shape, 3)
    cols = lax.broadcasted_iota(jnp.int32, shape, 4)
    return jnp.where(rows == cols, 0.15, 0.0) + 0.08 / math.sqrt(NEXT) * noise


def draw_coarse_inverse(key, part):
    key = jax.random.fold_in(key, 12)
    shape = (DK, DK)
    noise = jnp.clip(jax.random.normal(key, shape, jnp.float32), -4.0, 4.0)
    rows = lax.broadcasted_iota(jnp.int32, shape, 0)
    cols = lax.broadcasted_iota(jnp.int32, shape, 1)
    return jnp.where(rows == cols, 0.5, 0.0) + 0.5 / math.sqrt(DK) * noise


def draw_rhs(key, part):
    key = jax.random.fold_in(key, 13)
    first, second, third = jax.random.split(key, 3)
    shape = (N_GX, N_GY, N_GZ, OWN, NRHS)
    linear = lax.broadcasted_iota(jnp.float32, shape, 0) * (N_GY * N_GZ) + lax.broadcasted_iota(jnp.float32, shape, 1) * N_GZ + lax.broadcasted_iota(jnp.float32, shape, 2)
    ramp = jnp.exp(math.log(3.0) * linear / max(DEVICES - 1, 1))
    row_scale = jnp.exp(jax.random.uniform(first, (N_GX, N_GY, N_GZ, OWN, 1), jnp.float32, 0.0, math.log(10.0)))
    col_scale = jnp.exp(jax.random.uniform(second, (1, 1, 1, 1, NRHS), jnp.float32, 0.0, math.log(10.0)))
    noise = jnp.clip(jax.random.normal(third, shape, jnp.float32), -4.0, 4.0)
    return jnp.clip(0.1 * ramp * row_scale * col_scale * noise, -40.0, 40.0)


def with_ends(result, key, least, top_value):
    longest = result.shape.index(max(result.shape))
    spots = []
    for shift in (0, 1):
        where = [jax.random.randint(jax.random.fold_in(key, axis), (), 0, length) for axis, length in enumerate(result.shape)]
        where[longest] = (where[longest] + shift) % result.shape[longest]
        spots.append(tuple(where))
    return result.at[spots[0]].set(least).at[spots[1]].set(top_value)


def steps_of(stream_key, dims, shards, low, high):
    loudness = 1.0
    for dim, parts in shards:
        heights = jax.random.uniform(jax.random.fold_in(jax.random.fold_in(stream_key, 6), dim), (parts,), jnp.float32, low / len(shards), high / len(shards))
        loudness = loudness * jnp.repeat(jnp.exp(heights), dims[dim] // parts).reshape((-1,) + (1,) * (len(dims) - 1 - dim))
    return loudness


def normal_values(rng, shape, width, limit, cuts=(), kind=jnp.bfloat16):
    loudness = steps_of(rng, shape, cuts, -0.22, 0.18) if cuts else 1.0
    drawn = jax.random.normal(rng, shape, jnp.float32) * width * loudness
    return jnp.minimum(jnp.maximum(drawn, -limit), limit).astype(kind)


def setup_inputs(seed: int = 0) -> dict:
    keys = jax.random.split(jax.random.key(seed), 10)
    rhs = draw_rhs(jax.random.fold_in(keys[9], 71), 0)
    diagonal = jnp.clip(jnp.exp(math.log(1.0) - 2.9957323 * jax.random.uniform(keys[1], (N_GX, N_GY, N_GZ, OWN), jnp.float32) ** steps_of(keys[1], (N_GX, N_GY, N_GZ, OWN), ((0, 8), (1, 4), (2, 4)), -0.2, 0.2)), 0.05, 1.0)
    couple = jnp.clip(1.0 * jax.random.uniform(keys[2], (N_GX, N_GY, N_GZ, 6, OWN), jnp.float32) ** steps_of(keys[2], (N_GX, N_GY, N_GZ, 6, OWN), ((0, 8), (1, 4), (2, 4)), -0.2, 0.2), 0.0, 1.0)
    neighbours = with_ends(jax.random.randint(keys[3], (N_GX, N_GY, N_GZ, 6, OWN), 0, NEXT), jax.random.fold_in(keys[3], 1), 0, NEXT - 1).astype(jnp.int32)
    export_rows = with_ends(jax.random.randint(keys[4], (N_GX, N_GY, N_GZ, 6, OVR), 0, OWN), jax.random.fold_in(keys[4], 1), 0, OWN - 1).astype(jnp.int32)
    local_inverse = draw_local_inverse(jax.random.fold_in(keys[9], 71), 0)
    basis = normal_values(keys[6], (N_GX, N_GY, N_GZ, K, OWN), OWN ** -0.5, 0.1875, ((0, 8), (1, 4), (2, 4)), jnp.float32)
    coarse_inverse = draw_coarse_inverse(jax.random.fold_in(keys[9], 71), 0)
    owner = jax.random.permutation(keys[8], DEVICES).astype(jnp.int32)
    return dict(rhs=rhs, diagonal=diagonal, couple=couple, neighbours=neighbours, export_rows=export_rows, local_inverse=local_inverse, basis=basis, coarse_inverse=coarse_inverse, owner=owner)


def on_grid(function):
    return jax.vmap(jax.vmap(jax.vmap(function)))


def pick_rows(values, indices):
    return values[indices]


def product(left, right):
    return jnp.dot(left, right, precision=lax.Precision.HIGHEST)


def product_turned(left, right):
    return jnp.dot(left.T, right, precision=lax.Precision.HIGHEST)


def moved(blocks, axis, offset):
    length = blocks.shape[axis]
    empty = jnp.zeros_like(lax.slice_in_dim(blocks, 0, 1, axis=axis))
    if offset > 0:
        return jnp.concatenate([empty, lax.slice_in_dim(blocks, 0, length - 1, axis=axis)], axis=axis)
    return jnp.concatenate([lax.slice_in_dim(blocks, 1, length, axis=axis), empty], axis=axis)


def extended(field, export_rows):
    outgoing = on_grid(pick_rows)(field, export_rows)
    pieces = [field]
    for axis in range(3):
        pieces.append(moved(outgoing[:, :, :, 2 * axis + 1], axis, 1))
        pieces.append(moved(outgoing[:, :, :, 2 * axis], axis, -1))
    return jnp.concatenate(pieces, axis=3)


def operate(field, diagonal, couple, neighbours, export_rows):
    whole = extended(field, export_rows)
    picked = on_grid(pick_rows)(whole, neighbours)
    return (6.0 + diagonal)[..., None] * field - jnp.sum(couple[..., None] * picked, axis=3)


def reference(rhs, diagonal, couple, neighbours, export_rows, local_inverse, basis, coarse_inverse, owner):
    shape = rhs.shape
    members = shape[0] * shape[1] * shape[2]
    solution = jnp.zeros_like(rhs)
    residual = rhs
    for sweep in range(ITERS):
        local = on_grid(product)(local_inverse, extended(residual, export_rows))
        projected = on_grid(product)(basis, residual).reshape(members, K, NRHS)
        coarse = jnp.zeros_like(projected).at[owner].set(projected)
        solved = product(coarse_inverse, coarse.reshape(members * K, NRHS)).reshape(members, K, NRHS)
        mapped = solved[owner].reshape(shape[0], shape[1], shape[2], K, NRHS)
        update = local + on_grid(product_turned)(basis, mapped)
        image = operate(update, diagonal, couple, neighbours, export_rows)
        cross = jnp.sum(residual * image, axis=(0, 1, 2, 3))
        energy = jnp.sum(image * image, axis=(0, 1, 2, 3))
        alpha = cross / energy
        solution = solution + alpha * update
        residual = residual - alpha * image
    return solution, residual
```

```python
import jax
import jax.numpy as jnp
from jax import lax
from jax.experimental import pallas as pl
from jax.experimental.pallas import tpu as pltpu
from jax.sharding import PartitionSpec as P

F32 = jnp.float32
BF16 = jnp.bfloat16
MESH = pl.DeviceIdType.MESH

OWN = 1024
NRHS = 128
K = 64
OVR = 256
NEXT = 2560
CHIPS = 64
LCH = 128
NLCH = OWN // LCH
LSLOTS = 4

SHARES = ((0, 24, (2, 1, 0)), (24, 24, (0, 2, 1)), (48, 16, (1, 0, 2)))


def split(x):
    hi = x.astype(BF16)
    lo = (x - hi.astype(F32)).astype(BF16)
    return hi, lo


def put_pair(ref, start, x):
    hi, lo = split(x)
    rows = x.shape[0]
    ref[pl.ds(start, rows), 0:NRHS] = hi
    ref[pl.ds(start, rows), NRHS : 2 * NRHS] = lo


def dot(a, b):
    return jnp.dot(a, b, preferred_element_type=F32)


def dot_nt(a, b):
    return lax.dot_general(a, b, (((1,), (1,)), ((), ())), preferred_element_type=F32)


def fold(p, q):
    return p[:, 0:NRHS] + p[:, NRHS : 2 * NRHS] + q


def stacked(s, x):
    p = dot(s, x)
    half = s.shape[0] // 2
    return fold(p[0:half], p[half:, 0:NRHS])


def ring(v, n):
    return [v] + [lax.rem(v + d, n) for d in range(1, n)]


def kernel(
    rhs_h,
    diag_h,
    couple_h,
    links_h,
    exports_h,
    linv_h,
    basis_h,
    cinv_h,
    owner_s,
    owner_h,
    sol_ref,
    res_ref,
    rv,
    basis_v,
    diag_v,
    couple_v,
    links_v,
    exports_v,
    owner_v,
    lstage,
    linv,
    amat,
    emat,
    cinv_v,
    chl,
    csend,
    crecv,
    gat,
    xg,
    xhl,
    bcat,
    bt,
    bhl,
    msend,
    mrecv,
    l0,
    al0,
    u0,
    w0,
    l1,
    al1,
    gmat,
    hmat,
    sel,
    mhl,
    tcol,
    ncol,
    ecol,
    psrc,
    rbuf,
    sbuf,
    ssend,
    srecv,
    dsend,
    dsis,
    dpair,
    dall,
    in_sem,
    l_sem,
    g_ss,
    g_rs,
    m_ss,
    m_rs,
    c_sem,
    s_sem,
    d_sem,
):
    gx = lax.axis_index("gx")
    y = lax.axis_index("gy")
    z = lax.axis_index("gz")
    x, core = gx // 2, lax.rem(gx, 2)
    chip = (x * 4 + y) * 4 + z
    RX, RY, RZ = ring(x, 4), ring(y, 4), ring(z, 4)
    sister = (x * 2 + 1 - core, y, z)
    place = [x, y, z]

    def at(a, b, c):
        return (a * 2 + core, b, c)

    pending = []

    def send(src, dst, ssem, rsem, device):
        copy = pltpu.make_async_remote_copy(
            src_ref=src, dst_ref=dst, send_sem=ssem, recv_sem=rsem, device_id=device, device_id_type=MESH
        )
        copy.start()
        pending.append(copy)
        return copy

    loads = []
    for i, (src, dst) in enumerate(
        (
            (basis_h, basis_v),
            (rhs_h, rv),
            (exports_h, exports_v),
            (couple_h, couple_v),
            (links_h, links_v),
            (diag_h, diag_v),
            (owner_h, owner_v),
        )
    ):
        copy = pltpu.make_async_copy(src, dst, in_sem.at[i])
        copy.start()
        loads.append(copy)

    def load_columns(t):
        return pltpu.make_async_copy(cinv_h.at[:, pl.ds(pl.multiple_of(t * 128, 128), 128)], cinv_v.at[t], in_sem.at[7])

    def load_column(t, carry):
        load_columns(t).start()
        return carry

    lax.fori_loop(0, 64, load_column, 0)

    def load_chunk(c):
        return pltpu.make_async_copy(linv_h.at[pl.ds(c * LCH, LCH)], lstage.at[c % LSLOTS], l_sem.at[c % LSLOTS])

    for c in range(LSLOTS):
        load_chunk(c).start()

    far = []
    for d in range(1, CHIPS):
        a, b, c = RX[d // 16], RY[(d // 4) % 4], RZ[d % 4]
        far.append(((a * 4 + b) * 4 + c, at(a, b, c)))
    gx_up = (lax.rem(gx + 1, 8), y, z)
    gx_down = (lax.rem(gx + 7, 8), y, z)
    across = (lax.rem(gx + 7 + 2 * core, 8), y, z)
    bar = pltpu.get_barrier_semaphore()
    for _, device in far:
        pl.semaphore_signal(bar, inc=1, device_id=device, device_id_type=MESH)
    pl.semaphore_signal(bar, inc=1, device_id=sister, device_id_type=MESH)
    pl.semaphore_signal(bar, inc=1, device_id=across, device_id_type=MESH)

    def region(buf, order, stage, start, rows):
        index = [slice(None) if a in order[:stage] else place[a] for a in range(3)]
        return buf.at[index[0], index[1], index[2], pl.ds(start, rows), :]

    def along(axis, d):
        p = list(place)
        p[axis] = (RX, RY, RZ)[axis][d]
        return at(*p)

    def gather_start(n, stage):
        for t, (start, rows, order) in enumerate(SHARES):
            reg = region(gat.at[n], order, stage, start, rows)
            for j, d in enumerate((1, 3, 2)):
                send(reg, reg, g_ss.at[n, t, stage, j], g_rs.at[n, t, stage, j], along(order[stage], d))

    def gather_wait(n, stage):
        for t, (start, rows, order) in enumerate(SHARES):
            reg = region(gat.at[n], order, stage, start, rows)
            for j in range(3):
                pltpu.make_async_copy(reg, reg, g_rs.at[n, t, stage, j]).wait()

    steps = (
        (gx_up, gx_down),
        ((gx, RY[1], z), (gx, RY[3], z)),
        ((gx, y, RZ[1]), (gx, y, RZ[3])),
    )
    valid = []
    for coordinate, length in ((gx, 8), (y, 4), (z, 4)):
        valid.append(jnp.where(coordinate > 0, 1.0, 0.0).astype(F32))
        valid.append(jnp.where(coordinate < length - 1, 1.0, 0.0).astype(F32))

    def margins_start(n):
        for e in range(3):
            up, down = steps[e]
            send(msend.at[n, 2 * e + 1], mrecv.at[n, 2 * e], m_ss.at[n, 2 * e], m_rs.at[n, 2 * e], up)
            send(msend.at[n, 2 * e], mrecv.at[n, 2 * e + 1], m_ss.at[n, 2 * e + 1], m_rs.at[n, 2 * e + 1], down)

    def margins_wait(n):
        for b in range(6):
            pltpu.make_async_copy(mrecv.at[n, b], mrecv.at[n, b], m_rs.at[n, b]).wait()

    def outgoing(n):
        def step(d, carry):
            p = dot(emat[pl.ds(pl.multiple_of(d * OVR, OVR), OVR), :], xhl[0:OWN, :])
            msend[n, d] = p[:, 0:NRHS] + p[:, NRHS:]
            return carry

        lax.fori_loop(0, 6, step, 0)

    def import_margins(n):
        margins_wait(n)
        for b in range(6):
            put_pair(xhl, OWN + b * OVR, mrecv[n, b] * valid[b])

    def big_product(mat, dst):
        def step(i, carry):
            r = pl.multiple_of(i * 256, 256)
            p = dot(mat[0, pl.ds(r, 256), :], xhl[...])
            q = dot(mat[1, pl.ds(r, 256), :], xhl[:, 0:NRHS])
            dst[pl.ds(r, 256), :] = fold(p, q)
            return carry

        lax.fori_loop(0, OWN // 256, step, 0)

    def solve(n):
        total = jnp.zeros((256, 256), F32)
        for a in range(4):
            def chunk(b, carry):
                block = gat[n, a, b].reshape(256, NRHS)
                put_pair(xg, pl.multiple_of((a * 4 + b) * 256, 256), block)
                return carry

            lax.fori_loop(0, 4, chunk, 0)
            total = total + dot(chl[:, a * 1024 : (a + 1) * 1024], xg[a * 1024 : (a + 1) * 1024, :])
        res = total[0:128, 0:NRHS] + total[0:128, NRHS:] + total[128:256, 0:NRHS]
        psrc[n, 0] = res[0:64]
        psrc[n, 1] = res[64:128]

    def scatter_start(n):
        for c, device in far:
            copy = pltpu.make_async_remote_copy(
                src_ref=psrc.at[n, :, c, :],
                dst_ref=rbuf.at[n, :, chip, :],
                send_sem=s_sem.at[n, 0],
                recv_sem=s_sem.at[n, 1],
                device_id=device,
                device_id_type=MESH,
            )
            copy.start()
        rbuf[n, :, pl.ds(chip, 1), :] = psrc[n, :, pl.ds(chip, 1), :]

    def wait_all(ref, sem):
        pltpu.make_async_copy(ref, ref, sem).wait()

    def swap(n):
        wait_all(rbuf.at[n, :, pl.ds(0, 63), :], s_sem.at[n, 1])
        send(rbuf.at[n], sbuf.at[n], s_sem.at[n, 2], s_sem.at[n, 3], sister).wait_recv()
        first = rbuf[n, 0] + sbuf[n, 1]
        second = rbuf[n, 1] + sbuf[n, 0]
        hi, lo = split(jnp.concatenate([first, second], axis=0))
        p = dot(sel[...], jnp.concatenate([hi, lo], axis=1))
        ssend[n] = (p[:, 0:NRHS] + p[:, NRHS:]).reshape(CHIPS, 8, NRHS)
        for c, device in far:
            copy = pltpu.make_async_remote_copy(
                src_ref=ssend.at[n, c],
                dst_ref=srecv.at[n, chip],
                send_sem=s_sem.at[n, 4],
                recv_sem=s_sem.at[n, 5],
                device_id=device,
                device_id_type=MESH,
            )
            copy.start()
        srecv[n, chip] = ssend[n, chip]

    def mapped_in(n):
        wait_all(srecv.at[n, pl.ds(0, 63)], s_sem.at[n, 5])
        for s in range(8):
            put_pair(mhl, s * K, srecv[n, :, s, :])

    def scatter_drain(n):
        wait_all(rbuf.at[n, :, pl.ds(0, 63), :], s_sem.at[n, 0])
        wait_all(srecv.at[n, pl.ds(0, 63)], s_sem.at[n, 4])

    def add_coarse(base, dst):
        mine = mhl[6 * K : 7 * K, :]
        dst[...] = base[...] + fold(dot(bt[0], mine), dot(bt[1], mine[:, 0:NRHS]))

    def apply_coarse(base, dst):
        def step(i, carry):
            r = pl.multiple_of(i * 256, 256)
            p = dot(gmat[0, pl.ds(r, 256), :], mhl[...])
            q = dot(gmat[1, pl.ds(r, 256), :], mhl[:, 0:NRHS])
            dst[pl.ds(r, 256), :] = base[pl.ds(r, 256), :] + fold(p, q)
            return carry

        lax.fori_loop(0, OWN // 256, step, 0)

    def totals_start(n, left, right):
        dsend[n] = jnp.zeros((8, NRHS), F32)
        dsend[n, 0:1, :] = jnp.sum(left[...] * right[...], axis=0, keepdims=True)
        dsend[n, 1:2, :] = jnp.sum(right[...] * right[...], axis=0, keepdims=True)
        return send(dsend.at[n], dsis.at[n], d_sem.at[n, 0], d_sem.at[n, 1], sister)

    def totals_spread(n, copy):
        copy.wait_recv()
        dpair[n] = dsend[n] + dsis[n]
        for c, device in far:
            copy = pltpu.make_async_remote_copy(
                src_ref=dpair.at[n, pl.ds(0, 2)],
                dst_ref=dall.at[n, pl.ds(2 * chip, 2)],
                send_sem=d_sem.at[n, 2],
                recv_sem=d_sem.at[n, 3],
                device_id=device,
                device_id_type=MESH,
            )
            copy.start()
        dall[n, pl.ds(2 * chip, 2)] = dpair[n, 0:2]

    def totals_finish(n):
        wait_all(dall.at[n, pl.ds(0, 126)], d_sem.at[n, 3])
        cross = jnp.sum(dall[n, pl.ds(0, 64, stride=2), :], axis=0, keepdims=True)
        energy = jnp.sum(dall[n, pl.ds(1, 64, stride=2), :], axis=0, keepdims=True)
        wait_all(dall.at[n, pl.ds(0, 126)], d_sem.at[n, 2])
        return cross / energy

    loads[0].wait()
    loads[1].wait()
    put_pair(xhl, 0, rv[...])
    hi, lo = split(basis_v[...])
    bhl[0:K, :] = hi
    bhl[K : 2 * K, :] = lo
    gat[0, x, y, z] = stacked(bhl[...], xhl[0:OWN, :])
    pl.semaphore_wait(bar, CHIPS + 1)
    gather_start(0, 0)

    loads[2].wait()
    tcol[...] = jnp.zeros_like(tcol)
    ncol[...] = jnp.zeros_like(ncol)
    tcol[0:6, 0:256] = exports_v[...].astype(F32)
    ecol[...] = tcol[...][:, 0:256].T

    def export_rows(d, carry):
        def group(g, inner):
            rows = ecol[pl.ds(pl.multiple_of(g * 32, 32), 32), :]
            lane = lax.broadcasted_iota(jnp.int32, (32, 8), 1)
            col = jnp.sum(jnp.where(lane == d, rows, 0.0), axis=1, keepdims=True).astype(jnp.int32)
            cells = lax.broadcasted_iota(jnp.int32, (32, OWN), 1)
            emat[pl.ds(pl.multiple_of(d * OVR + g * 32, 32), 32), :] = jnp.where(cells == col, 1.0, 0.0).astype(BF16)
            return inner

        return lax.fori_loop(0, OVR // 32, group, carry)

    lax.fori_loop(0, 6, export_rows, 0)
    outgoing(0)
    margins_start(0)

    pltpu.make_async_copy(cinv_v, cinv_v, in_sem.at[7]).wait()
    lane = lax.broadcasted_iota(jnp.int32, (K, 128), 1)

    def column_block(c, kk, half):
        cx, cy, cz = c // 16, lax.rem(c // 4, 4), lax.rem(c, 4)
        j = owner_s[((cx * 2 + kk) * 4 + cy) * 4 + cz]
        pair = lax.shift_right_logical(j, 1)
        tile = cinv_v[pair]
        turned = pltpu.roll(tile, 64, 1)
        same = jnp.full((K, 128), j - 2 * pair, jnp.int32) == half
        return jnp.where(same, tile, turned)

    def column_pair(m, kk):
        return jnp.where(lane < 64, column_block(2 * m, kk, 0), column_block(2 * m + 1, kk, 1))

    def order_other(m, carry):
        csend[:, pl.ds(pl.multiple_of(m * 128, 128), 128)] = column_pair(m, 1 - core)
        return carry

    def order_mine(m, carry):
        hi, lo = split(column_pair(m, core))
        chl[0:64, pl.ds(pl.multiple_of(m * 128, 128), 128)] = hi
        chl[128:192, pl.ds(pl.multiple_of(m * 128, 128), 128)] = lo
        return carry

    lax.fori_loop(0, 32, order_other, 0)
    ccopy = send(csend, crecv, c_sem.at[0], c_sem.at[1], sister)
    gather_wait(0, 0)
    gather_start(0, 1)
    lax.fori_loop(0, 32, order_mine, 0)

    bcat[0, 0:K, :] = bhl[0:K, :]
    bcat[0, K : 2 * K, :] = bhl[0:K, :]
    bcat[1, 0:K, :] = bhl[K : 2 * K, :]
    bcat[1, K : 2 * K, :] = bhl[K : 2 * K, :]

    def export_basis(d, carry):
        rows = emat[pl.ds(pl.multiple_of(d * OVR, OVR), OVR), :]
        msend[1, d] = dot_nt(rows, bcat[0]) + dot_nt(rows, bcat[1])
        return carry

    lax.fori_loop(0, 6, export_basis, 0)
    gather_wait(0, 1)
    gather_start(0, 2)
    margins_start(1)

    for c in range(NLCH):
        load_chunk(c).wait()

        def halves(g, carry):
            r = pl.multiple_of(g * 16, 16)
            hi, lo = split(lstage[c % LSLOTS, pl.ds(r, 16), :])
            linv[0, pl.ds(c * LCH + r, 16), :] = hi
            linv[1, pl.ds(c * LCH + r, 16), :] = lo
            return carry

        lax.fori_loop(0, LCH // 16, halves, 0)
        if c + LSLOTS < NLCH:
            load_chunk(c + LSLOTS).start()

    import_margins(0)
    big_product(linv, l0)
    put_pair(xhl, 0, l0[...])
    outgoing(2)
    margins_start(2)

    for i in (3, 4, 5):
        loads[i].wait()
    tcol[0:6, :] = couple_v[...]
    tcol[6:7, :] = diag_v[...] + 6.0
    ncol[0:6, :] = links_v[...].astype(F32)
    al0[:, 0:8] = tcol[...].T
    al0[:, 8:16] = ncol[...].T

    def operator_rows(g, carry):
        r = pl.multiple_of(g * 16, 16)
        cols = al0[pl.ds(r, 16), 0:16]
        weights = [cols[:, k : k + 1] for k in range(7)]
        targets = [cols[:, 8 + k : 9 + k].astype(jnp.int32) for k in range(6)]
        own = lax.broadcasted_iota(jnp.int32, (16, 1), 0) + r
        for start in range(0, NEXT, 512):
            cells = lax.broadcasted_iota(jnp.int32, (16, 512), 1) + start
            acc = jnp.zeros((16, 512), F32)
            if start < OWN:
                acc = jnp.where(cells == own, weights[6], 0.0)
            for k in range(6):
                acc = acc - jnp.where(cells == targets[k], weights[k], 0.0)
            hi, lo = split(acc)
            amat[0, pl.ds(r, 16), start : start + 512] = hi
            amat[1, pl.ds(r, 16), start : start + 512] = lo
        return carry

    lax.fori_loop(0, OWN // 16, operator_rows, 0)

    ccopy.wait_recv()

    def sister_rows(m, carry):
        cols = pl.ds(pl.multiple_of(m * 128, 128), 128)
        hi, lo = split(crecv[:, cols])
        chl[64:128, cols] = hi
        chl[192:256, cols] = lo
        return carry

    lax.fori_loop(0, 32, sister_rows, 0)
    gather_wait(0, 2)
    solve(0)
    scatter_start(0)

    margins_wait(1)
    basis_t = basis_v[...].T
    hi, lo = split(basis_t)
    bt[0] = hi
    bt[1] = lo
    hi, lo = split(jnp.concatenate([basis_t, jnp.zeros_like(basis_t)], axis=1))
    xg[0:OWN, 0:128] = hi
    xg[0:OWN, 128:256] = lo
    lane_v = lax.broadcasted_iota(jnp.int32, (OVR, 128), 1)
    for b in range(6):
        mask = jnp.where((lane_v < 64) == (b % 2 == 0), valid[b], 0.0)
        put_pair(xg, OWN + b * OVR, mrecv[1, b] * mask)

    def coarse_columns(i, carry):
        r = pl.multiple_of(i * 256, 256)
        for j in range(4):
            rows = slice(0, OWN) if j == 3 else slice(OWN + j * 512, OWN + (j + 1) * 512)
            p = dot(amat[0, pl.ds(r, 256), rows], xg[rows, :])
            q = dot(amat[1, pl.ds(r, 256), rows], xg[rows, 0:NRHS])
            hi, lo = split(fold(p, q))
            gmat[0, pl.ds(r, 256), j * 128 : (j + 1) * 128] = hi
            gmat[1, pl.ds(r, 256), j * 128 : (j + 1) * 128] = lo
        return carry

    lax.fori_loop(0, OWN // 256, coarse_columns, 0)
    p = dot(bhl[...], gmat[0])
    h = p[0:K] + p[K:] + dot(bhl[0:K, :], gmat[1])
    hi, lo = split(h)
    hmat[0:K, :] = hi
    hmat[K : 2 * K, :] = lo

    loads[6].wait()
    r_ = lax.broadcasted_iota(jnp.int32, (512, 128), 0)
    q_ = lax.broadcasted_iota(jnp.int32, (512, 128), 1)
    c_, s_ = r_ // 8, r_ % 8
    dx = jnp.where(s_ == 0, 7, jnp.where(s_ == 1, 1, 0))
    dy = jnp.where(s_ == 2, 3, jnp.where(s_ == 3, 1, 0))
    dz = jnp.where(s_ == 4, 3, jnp.where(s_ == 5, 1, 0))
    px = ((c_ // 16) * 2 + core + dx) % 8
    py = ((c_ // 4) % 4 + dy) % 4
    pz = (c_ % 4 + dz) % 4
    wanted = jnp.where(q_ == (px * 4 + py) * 4 + pz, 1.0, 0.0).astype(BF16)
    i_ = lax.broadcasted_iota(jnp.int32, (128, 128), 0)
    ch_ = i_ % 64
    kk_ = (core + i_ // 64) % 2
    block = (((ch_ // 16) * 2 + kk_) * 4 + (ch_ // 4) % 4) * 4 + ch_ % 4
    held = jnp.where(owner_v[...] == block, 1.0, 0.0).astype(BF16)
    sel[...] = dot_nt(wanted, held).astype(BF16)

    swap(0)
    import_margins(2)
    big_product(amat, al0)
    put_pair(xhl, 0, al0[...])
    projected = stacked(bhl[...], xhl[0:OWN, :])
    mapped_in(0)

    gat[1, x, y, z] = projected + stacked(hmat[...], mhl[...])
    gather_start(1, 0)
    apply_coarse(al0, w0)
    put_pair(xhl, 0, w0[...])
    outgoing(3)
    margins_start(3)
    dots = totals_start(0, rv, w0)
    gather_wait(1, 0)
    gather_start(1, 1)
    totals_spread(0, dots)
    add_coarse(l0, u0)
    gather_wait(1, 1)
    gather_start(1, 2)
    import_margins(3)
    big_product(linv, l1)
    put_pair(xhl, 0, l1[...])
    outgoing(4)
    margins_start(4)
    alpha0 = totals_finish(0)
    rv[...] = rv[...] - alpha0 * w0[...]
    import_margins(4)
    big_product(amat, al1)
    gather_wait(1, 2)
    solve(1)
    scatter_start(1)
    swap(1)
    mapped_in(1)
    apply_coarse(al1, al1)
    w0[...] = w0[...] - alpha0 * al1[...]
    dots = totals_start(1, rv, w0)
    totals_spread(1, dots)
    add_coarse(l1, l1)
    l1[...] = u0[...] - alpha0 * l1[...]
    alpha1 = totals_finish(1)
    sol_ref[...] = alpha0 * u0[...] + alpha1 * l1[...]
    res_ref[...] = rv[...] - alpha1 * w0[...]

    for copy in pending:
        copy.wait_send()
    scatter_drain(0)
    scatter_drain(1)


def run(rhs, diagonal, couple, links, exports, linv, basis, cinv, owner):
    field = (OWN, NRHS)
    dma = pltpu.SemaphoreType.DMA
    vm = pltpu.VMEM
    scratch = [
        vm(field, F32),
        vm((K, OWN), F32),
        vm((1, OWN), F32),
        vm((6, OWN), F32),
        vm((6, OWN), jnp.int32),
        vm((6, OVR), jnp.int32),
        vm((1, 128), jnp.int32),
        vm((LSLOTS, LCH, NEXT), F32),
        vm((2, OWN, NEXT), BF16),
        vm((2, OWN, NEXT), BF16),
        vm((6 * OVR, OWN), BF16),
        vm((64, K, 128), F32),
        vm((256, 4096), BF16),
        vm((K, 4096), F32),
        vm((K, 4096), F32),
        vm((2, 4, 4, 4, K, NRHS), F32),
        vm((4096, 256), BF16),
        vm((NEXT, 256), BF16),
        vm((2, 128, OWN), BF16),
        vm((2, OWN, K), BF16),
        vm((128, OWN), BF16),
        vm((5, 6, OVR, NRHS), F32),
        vm((5, 6, OVR, NRHS), F32),
        vm(field, F32),
        vm(field, F32),
        vm(field, F32),
        vm(field, F32),
        vm(field, F32),
        vm(field, F32),
        vm((2, OWN, 512), BF16),
        vm((128, 512), BF16),
        vm((512, 128), BF16),
        vm((512, 256), BF16),
        vm((8, OWN), F32),
        vm((8, OWN), F32),
        vm((OVR, 8), F32),
        vm((2, 2, CHIPS, NRHS), F32),
        vm((2, 2, CHIPS, NRHS), F32),
        vm((2, 2, CHIPS, NRHS), F32),
        vm((2, CHIPS, 8, NRHS), F32),
        vm((2, CHIPS, 8, NRHS), F32),
        vm((2, 8, NRHS), F32),
        vm((2, 8, NRHS), F32),
        vm((2, 8, NRHS), F32),
        vm((2, 128, NRHS), F32),
        dma((8,)),
        dma((LSLOTS,)),
        dma((2, 3, 3, 3)),
        dma((2, 3, 3, 3)),
        dma((5, 6)),
        dma((5, 6)),
        dma((2,)),
        dma((2, 6)),
        dma((2, 4)),
    ]
    anywhere = pl.BlockSpec(memory_space=pl.ANY)
    return pl.pallas_call(
        kernel,
        out_shape=(jax.ShapeDtypeStruct(field, F32), jax.ShapeDtypeStruct(field, F32)),
        in_specs=[anywhere] * 8 + [pl.BlockSpec(memory_space=pltpu.SMEM), anywhere],
        out_specs=(pl.BlockSpec(memory_space=pltpu.VMEM), pl.BlockSpec(memory_space=pltpu.VMEM)),
        scratch_shapes=scratch,
        compiler_params=pltpu.CompilerParams(
            collective_id=0, has_side_effects=True, vmem_limit_bytes=63 * 1024 * 1024
        ),
        cost_estimate=pl.CostEstimate(flops=12_000_000_000, bytes_accessed=15_000_000, transcendentals=0),
    )(rhs, diagonal, couple, links, exports, linv, basis, cinv, owner, owner.reshape(1, 128))


def body(rhs, diagonal, couple, neighbours, export_rows, local_inverse, basis, coarse_inverse, owner):
    solution, residual = run(
        rhs.reshape(OWN, NRHS),
        diagonal.reshape(1, OWN),
        couple.reshape(6, OWN),
        neighbours.reshape(6, OWN),
        export_rows.reshape(6, OVR),
        local_inverse.reshape(OWN, NEXT),
        basis.reshape(K, OWN),
        coarse_inverse,
        owner,
    )
    return solution.reshape(rhs.shape), residual.reshape(rhs.shape)


def solution(mesh):
    placed = (
        P("gx", "gy", "gz", None, None),
        P("gx", "gy", "gz", None),
        P("gx", "gy", "gz", None, None),
        P("gx", "gy", "gz", None, None),
        P("gx", "gy", "gz", None, None),
        P("gx", "gy", "gz", None, None),
        P("gx", "gy", "gz", None, None),
        P(("gx", "gy", "gz"), None),
        P(),
    )
    return jax.shard_map(
        body,
        mesh=mesh,
        in_specs=placed,
        out_specs=(P("gx", "gy", "gz", None, None), P("gx", "gy", "gz", None, None)),
        check_vma=False,
    )
```

```python
import jax
import jax.numpy as jnp
from jax import lax
from jax.experimental import pallas as pl
from jax.experimental.pallas import tpu as pltpu
from jax.sharding import PartitionSpec as P

F32 = jnp.float32
BF16 = jnp.bfloat16
MESH = pl.DeviceIdType.MESH

OWN = 1024
NRHS = 128
K = 64
OVR = 256
NEXT = 2560
CHIPS = 64
LCH = 128
NLCH = OWN // LCH
LSLOTS = 4

SHARES = ((0, 24, (2, 1, 0)), (24, 24, (0, 2, 1)), (48, 16, (1, 0, 2)))


def split(x):
    hi = x.astype(BF16)
    lo = (x - hi.astype(F32)).astype(BF16)
    return hi, lo


def put_pair(ref, start, x):
    hi, lo = split(x)
    rows = x.shape[0]
    ref[pl.ds(start, rows), 0:NRHS] = hi
    ref[pl.ds(start, rows), NRHS : 2 * NRHS] = lo


def dot(a, b):
    return jnp.dot(a, b, preferred_element_type=F32)


def dot_nt(a, b):
    return lax.dot_general(a, b, (((1,), (1,)), ((), ())), preferred_element_type=F32)


def fold(p, q):
    return p[:, 0:NRHS] + p[:, NRHS : 2 * NRHS] + q


def stacked(s, x):
    p = dot(s, x)
    half = s.shape[0] // 2
    return fold(p[0:half], p[half:, 0:NRHS])


def ring(v, n):
    return [v] + [lax.rem(v + d, n) for d in range(1, n)]


def hops(d):
    return sum((0, 1, 2, 1)[i] for i in (d // 16, (d // 4) % 4, d % 4))


def kernel(
    rhs_h,
    diag_h,
    couple_h,
    links_h,
    exports_h,
    linv_h,
    basis_h,
    cinv_h,
    owner_s,
    owner_h,
    sol_ref,
    update_ref,
    res_ref,
    image_ref,
    alpha_ref,
    rv,
    basis_v,
    diag_v,
    couple_v,
    links_v,
    exports_v,
    owner_v,
    lstage,
    linv,
    amat,
    emat,
    cinv_v,
    chl,
    csend,
    crecv,
    gat,
    xg,
    xhl,
    bcat,
    bt,
    bhl,
    msend,
    mrecv,
    bsend,
    brecv,
    l0,
    al0,
    u0,
    w0,
    l1,
    al1,
    gmat,
    hmat,
    sel,
    mhl,
    tcol,
    ncol,
    ecol,
    psrc,
    rbuf,
    sbuf,
    ssend,
    srecv,
    dsend,
    dsis,
    dpair,
    dall,
    in_sem,
    l_sem,
    g_ss,
    g_rs,
    m_ss,
    m_rs,
    c_sem,
    s_sem,
    d_sem,
    out_sem,
):
    gx = lax.axis_index("gx")
    y = lax.axis_index("gy")
    z = lax.axis_index("gz")
    x, core = gx // 2, lax.rem(gx, 2)
    chip = (x * 4 + y) * 4 + z
    RX, RY, RZ = ring(x, 4), ring(y, 4), ring(z, 4)
    sister = (x * 2 + 1 - core, y, z)
    place = [x, y, z]

    def at(a, b, c):
        return (a * 2 + core, b, c)

    def along(axis, d):
        p = list(place)
        p[axis] = (RX, RY, RZ)[axis][d]
        return at(*p)

    pending = []

    def send(src, dst, ssem, rsem, device):
        copy = pltpu.make_async_remote_copy(
            src_ref=src, dst_ref=dst, send_sem=ssem, recv_sem=rsem, device_id=device, device_id_type=MESH
        )
        copy.start()
        pending.append(copy)
        return copy

    loads = []
    for i, (src, dst) in enumerate(
        (
            (basis_h, basis_v),
            (rhs_h, rv),
            (exports_h, exports_v),
            (couple_h, couple_v),
            (links_h, links_v),
            (diag_h, diag_v),
            (owner_h, owner_v),
        )
    ):
        copy = pltpu.make_async_copy(src, dst, in_sem.at[i])
        copy.start()
        loads.append(copy)

    def load_columns(t):
        return pltpu.make_async_copy(cinv_h.at[:, pl.ds(pl.multiple_of(t * 128, 128), 128)], cinv_v.at[t], in_sem.at[7])

    def load_column(t, carry):
        load_columns(t).start()
        return carry

    lax.fori_loop(0, 64, load_column, 0)

    def load_chunk(c):
        return pltpu.make_async_copy(linv_h.at[pl.ds(c * LCH, LCH)], lstage.at[c % LSLOTS], l_sem.at[c % LSLOTS])

    for c in range(LSLOTS):
        load_chunk(c).start()

    far = []
    for d in sorted(range(1, CHIPS), key=hops, reverse=True):
        a, b, c = RX[d // 16], RY[(d // 4) % 4], RZ[d % 4]
        far.append(((a * 4 + b) * 4 + c, at(a, b, c)))
    gx_up = (lax.rem(gx + 1, 8), y, z)
    gx_down = (lax.rem(gx + 7, 8), y, z)
    across = (lax.rem(gx + 7 + 2 * core, 8), y, z)
    bar = pltpu.get_barrier_semaphore()
    near = [along(axis, d) for d in (2, 1, 3) for axis in range(3)] + [across, sister]
    for device in near:
        pl.semaphore_signal(bar, inc=1, device_id=device, device_id_type=MESH)

    def region(n, t, stage, line=0):
        start, rows, order = SHARES[t]
        index = [slice(None) if a in order[:stage] else place[a] for a in range(3)]
        if stage == 2:
            axis = order[1]
            index[axis] = (RX, RY, RZ)[axis][line]
        return gat.at[n].at[index[0], index[1], index[2], pl.ds(start, rows), :]

    def gather_send(n, stage, line=0):
        slot = stage + line
        for t in range(3):
            reg = region(n, t, stage, line)
            for j, d in enumerate((1, 3, 2)):
                send(reg, reg, g_ss.at[n, t, slot, j], g_rs.at[n, t, slot, j], along(SHARES[t][2][stage], d))

    def gather_recv(n, stage, line=0):
        for t in range(3):
            reg = region(n, t, stage, line)
            for j in range(3):
                pltpu.make_async_copy(reg, reg, g_rs.at[n, t, stage + line, j]).wait()

    def gather_one(n):
        gather_send(n, 0)

    def gather_two(n):
        gather_recv(n, 0)
        gather_send(n, 1)
        gather_send(n, 2, 0)

    def gather_three(n):
        gather_recv(n, 1)
        for line in (1, 3, 2):
            gather_send(n, 2, line)

    def gather_done(n):
        for line in (0, 1, 3, 2):
            gather_recv(n, 2, line)

    steps = (
        (gx_up, gx_down),
        ((gx, RY[1], z), (gx, RY[3], z)),
        ((gx, y, RZ[1]), (gx, y, RZ[3])),
    )
    valid = []
    for coordinate, length in ((gx, 8), (y, 4), (z, 4)):
        valid.append(jnp.where(coordinate > 0, 1.0, 0.0).astype(F32))
        valid.append(jnp.where(coordinate < length - 1, 1.0, 0.0).astype(F32))

    def margins(n):
        return (bsend, brecv) if n == 1 else (msend.at[n if n == 0 else n - 1], mrecv.at[n if n == 0 else n - 1])

    def margins_start(n):
        out, into = margins(n)
        for e in range(3):
            up, down = steps[e]
            send(out.at[2 * e + 1], into.at[2 * e], m_ss.at[n, 2 * e], m_rs.at[n, 2 * e], up)
            send(out.at[2 * e], into.at[2 * e + 1], m_ss.at[n, 2 * e + 1], m_rs.at[n, 2 * e + 1], down)

    def margins_wait(n):
        into = margins(n)[1]
        for b in range(6):
            pltpu.make_async_copy(into.at[b], into.at[b], m_rs.at[n, b]).wait()

    def outgoing(n):
        out = margins(n)[0]

        def step(d, carry):
            p = dot(emat[pl.ds(pl.multiple_of(d * OVR, OVR), OVR), :], xhl[0:OWN, :])
            out[d] = p[:, 0:NRHS] + p[:, NRHS:]
            return carry

        lax.fori_loop(0, 6, step, 0)

    def import_margins(n):
        margins_wait(n)
        into = margins(n)[1]
        for b in range(6):
            put_pair(xhl, OWN + b * OVR, into[b] * valid[b])

    def big_product(mat, dst):
        def step(i, carry):
            r = pl.multiple_of(i * 512, 512)
            p = dot(mat[0, pl.ds(r, 512), :], xhl[...])
            q = dot(mat[1, pl.ds(r, 512), :], xhl[:, 0:NRHS])
            dst[pl.ds(r, 512), :] = fold(p, q)
            return carry

        lax.fori_loop(0, OWN // 512, step, 0)

    def solve(n):
        total = jnp.zeros((256, 256), F32)
        for a in range(4):
            for b in range(4):
                put_pair(xg, (a * 4 + b) * 256, gat[n, a, b].reshape(256, NRHS))
            total = total + dot(chl[:, a * 1024 : (a + 1) * 1024], xg[a * 1024 : (a + 1) * 1024, :])
        res = total[0:128, 0:NRHS] + total[0:128, NRHS:] + total[128:256, 0:NRHS]
        psrc[n, 0] = res[0:64]
        psrc[n, 1] = res[64:128]

    def scatter_start(n):
        for c, device in far:
            copy = pltpu.make_async_remote_copy(
                src_ref=psrc.at[n, :, c, :],
                dst_ref=rbuf.at[n, :, chip, :],
                send_sem=s_sem.at[n, 0],
                recv_sem=s_sem.at[n, 1],
                device_id=device,
                device_id_type=MESH,
            )
            copy.start()
        rbuf[n, :, pl.ds(chip, 1), :] = psrc[n, :, pl.ds(chip, 1), :]

    def wait_all(ref, sem):
        pltpu.make_async_copy(ref, ref, sem).wait()

    def swap(n):
        wait_all(rbuf.at[n, :, pl.ds(0, 63), :], s_sem.at[n, 1])
        send(rbuf.at[n], sbuf.at[n], s_sem.at[n, 2], s_sem.at[n, 3], sister).wait_recv()
        first = rbuf[n, 0] + sbuf[n, 1]
        second = rbuf[n, 1] + sbuf[n, 0]
        hi, lo = split(jnp.concatenate([first, second], axis=0))
        p = dot(sel[...], jnp.concatenate([hi, lo], axis=1))
        ssend[n] = (p[:, 0:NRHS] + p[:, NRHS:]).reshape(CHIPS, 8, NRHS)
        for c, device in far:
            copy = pltpu.make_async_remote_copy(
                src_ref=ssend.at[n, c, pl.ds(0, 7)],
                dst_ref=srecv.at[n, chip, pl.ds(0, 7)],
                send_sem=s_sem.at[n, 4],
                recv_sem=s_sem.at[n, 5],
                device_id=device,
                device_id_type=MESH,
            )
            copy.start()
        srecv[n, chip, 0:7] = ssend[n, chip, 0:7]

    def mapped_in(n):
        wait_all(srecv.at[n, pl.ds(0, 63), pl.ds(0, 7)], s_sem.at[n, 5])
        for s in range(7):
            put_pair(mhl, s * K, srecv[n, :, s, :])

    def scatter_drain(n):
        wait_all(rbuf.at[n, :, pl.ds(0, 63), :], s_sem.at[n, 0])
        wait_all(srecv.at[n, pl.ds(0, 63), pl.ds(0, 7)], s_sem.at[n, 4])

    def add_coarse(base, dst):
        mine = mhl[6 * K : 7 * K, :]
        dst[...] = base[...] + fold(dot(bt[0], mine), dot(bt[1], mine[:, 0:NRHS]))

    def apply_coarse(base, dst):
        def step(i, carry):
            r = pl.multiple_of(i * 256, 256)
            p = dot(gmat[0, pl.ds(r, 256), :], mhl[...])
            q = dot(gmat[1, pl.ds(r, 256), :], mhl[:, 0:NRHS])
            dst[pl.ds(r, 256), :] = base[pl.ds(r, 256), :] + fold(p, q)
            return carry

        lax.fori_loop(0, OWN // 256, step, 0)

    def totals_start(n, left, right):
        dsend[n] = jnp.zeros((8, NRHS), F32)
        dsend[n, 0:1, :] = jnp.sum(left[...] * right[...], axis=0, keepdims=True)
        dsend[n, 1:2, :] = jnp.sum(right[...] * right[...], axis=0, keepdims=True)
        return send(dsend.at[n], dsis.at[n], d_sem.at[n, 0], d_sem.at[n, 1], sister)

    def totals_spread(n, copy):
        copy.wait_recv()
        dpair[n] = dsend[n] + dsis[n]
        for c, device in far:
            copy = pltpu.make_async_remote_copy(
                src_ref=dpair.at[n, pl.ds(0, 2)],
                dst_ref=dall.at[n, pl.ds(2 * chip, 2)],
                send_sem=d_sem.at[n, 2],
                recv_sem=d_sem.at[n, 3],
                device_id=device,
                device_id_type=MESH,
            )
            copy.start()
        dall[n, pl.ds(2 * chip, 2)] = dpair[n, 0:2]

    def totals_finish(n):
        wait_all(dall.at[n, pl.ds(0, 126)], d_sem.at[n, 3])
        cross = jnp.sum(dall[n, pl.ds(0, 64, stride=2), :], axis=0, keepdims=True)
        energy = jnp.sum(dall[n, pl.ds(1, 64, stride=2), :], axis=0, keepdims=True)
        wait_all(dall.at[n, pl.ds(0, 126)], d_sem.at[n, 2])
        return cross / energy

    mhl[7 * K :, :] = jnp.zeros((K, 2 * NRHS), BF16)
    loads[0].wait()
    loads[1].wait()
    put_pair(xhl, 0, rv[...])
    hi, lo = split(basis_v[...])
    bhl[0:K, :] = hi
    bhl[K : 2 * K, :] = lo
    gat[0, x, y, z] = stacked(bhl[...], xhl[0:OWN, :])

    loads[2].wait()
    tcol[...] = jnp.zeros_like(tcol)
    ncol[...] = jnp.zeros_like(ncol)
    for d in range(6):
        tcol[d : d + 1, 0:OVR] = exports_v[d].astype(F32)
    ecol[...] = tcol[...][:, 0:OVR].T

    def export_rows(d, carry):
        def group(g, inner):
            rows = ecol[pl.ds(pl.multiple_of(g * 32, 32), 32), :]
            lane = lax.broadcasted_iota(jnp.int32, (32, 8), 1)
            col = jnp.sum(jnp.where(lane == d, rows, 0.0), axis=1, keepdims=True).astype(jnp.int32)
            cells = lax.broadcasted_iota(jnp.int32, (32, OWN), 1)
            emat[pl.ds(pl.multiple_of(d * OVR + g * 32, 32), 32), :] = jnp.where(cells == col, 1.0, 0.0).astype(BF16)
            return inner

        return lax.fori_loop(0, OVR // 32, group, carry)

    lax.fori_loop(0, 6, export_rows, 0)

    pltpu.make_async_copy(cinv_v, cinv_v, in_sem.at[7]).wait()
    lane = lax.broadcasted_iota(jnp.int32, (K, 128), 1)

    def column_block(c, kk, half):
        cx, cy, cz = c // 16, lax.rem(c // 4, 4), lax.rem(c, 4)
        j = owner_s[((cx * 2 + kk) * 4 + cy) * 4 + cz]
        pair = lax.shift_right_logical(j, 1)
        tile = cinv_v[pair]
        turned = pltpu.roll(tile, 64, 1)
        same = jnp.full((K, 128), j - 2 * pair, jnp.int32) == half
        return jnp.where(same, tile, turned)

    def column_pair(m, kk):
        return jnp.where(lane < 64, column_block(2 * m, kk, 0), column_block(2 * m + 1, kk, 1))

    def order_other(m, carry):
        csend[:, pl.ds(pl.multiple_of(m * 128, 128), 128)] = column_pair(m, 1 - core)
        return carry

    def order_mine(m, carry):
        hi, lo = split(column_pair(m, core))
        chl[0:64, pl.ds(pl.multiple_of(m * 128, 128), 128)] = hi
        chl[128:192, pl.ds(pl.multiple_of(m * 128, 128), 128)] = lo
        return carry

    lax.fori_loop(0, 32, order_other, 0)

    for i in (3, 4, 5):
        loads[i].wait()
    own_row = lax.broadcasted_iota(jnp.int32, (1, OWN), 1)
    targets = [links_v[k] for k in range(6)]
    weights = [couple_v[k] for k in range(6)]
    centre = diag_v[...] + 6.0
    for k in range(6):
        centre = centre - jnp.where(targets[k] == own_row, weights[k], 0.0)
        gone = targets[k] == own_row
        total = weights[k]
        for m in range(6):
            if m < k:
                gone = gone | (targets[m] == targets[k])
            if m > k:
                total = total + jnp.where(targets[m] == targets[k], weights[m], 0.0)
        tcol[k : k + 1, :] = -total
        ncol[k : k + 1, :] = jnp.where(gone, -1, targets[k]).astype(F32)
    tcol[6:7, :] = centre
    ncol[6:7, :] = own_row.astype(F32)
    al0[:, 0:8] = tcol[...].T
    al0[:, 8:16] = ncol[...].T

    def operator_rows(g, carry):
        r = pl.multiple_of(g * 16, 16)
        cols = al0[pl.ds(r, 16), 0:16]
        values = [split(jnp.broadcast_to(cols[:, k : k + 1], (16, 128))) for k in range(7)]
        places = [
            jnp.broadcast_to(cols[:, 8 + k : 9 + k], (16, 128)).astype(jnp.int32).astype(jnp.int16) for k in range(7)
        ]
        lanes = lax.broadcasted_iota(jnp.int32, (16, 128), 1)
        for j in range(NEXT // 128):
            cells = (lanes + j * 128).astype(jnp.int16)
            hi = jnp.zeros((16, 128), BF16)
            lo = jnp.zeros((16, 128), BF16)
            for k in range(7 if j < OWN // 128 else 6):
                hit = cells == places[k]
                hi = jnp.where(hit, values[k][0], hi)
                lo = jnp.where(hit, values[k][1], lo)
            amat[0, pl.ds(r, 16), j * 128 : (j + 1) * 128] = hi
            amat[1, pl.ds(r, 16), j * 128 : (j + 1) * 128] = lo
        return carry

    def build_operator(first, last):
        lax.fori_loop(first, last, operator_rows, 0)

    pl.semaphore_wait(bar, len(near))
    gather_one(0)
    ccopy = send(csend, crecv, c_sem.at[0], c_sem.at[1], sister)
    outgoing(0)
    margins_start(0)
    build_operator(0, 6)
    gather_two(0)
    lax.fori_loop(0, 32, order_mine, 0)
    build_operator(6, 18)
    gather_three(0)

    for c in range(NLCH):
        load_chunk(c).wait()

        def halves(g, carry):
            r = pl.multiple_of(g * 16, 16)
            hi, lo = split(lstage[c % LSLOTS, pl.ds(r, 16), :])
            linv[0, pl.ds(c * LCH + r, 16), :] = hi
            linv[1, pl.ds(c * LCH + r, 16), :] = lo
            return carry

        lax.fori_loop(0, LCH // 16, halves, 0)
        if c + LSLOTS < NLCH:
            load_chunk(c + LSLOTS).start()

    import_margins(0)
    big_product(linv, l0)
    put_pair(xhl, 0, l0[...])
    outgoing(2)
    build_operator(18, 40)

    bcat[0, 0:K, :] = bhl[0:K, :]
    bcat[0, K : 2 * K, :] = bhl[0:K, :]
    bcat[1, 0:K, :] = bhl[K : 2 * K, :]
    bcat[1, K : 2 * K, :] = bhl[K : 2 * K, :]
    lane_h = lax.broadcasted_iota(jnp.int32, (128, 128), 1)

    def export_basis(d, carry):
        rows = emat[pl.ds(pl.multiple_of(d * OVR, OVR), OVR), :]
        p = dot_nt(rows, bcat[0]) + dot_nt(rows, bcat[1])
        bsend[d] = jnp.where(lane_h < 64, p[0:128], p[128:256])
        return carry

    lax.fori_loop(0, 6, export_basis, 0)
    ccopy.wait_recv()

    def sister_rows(m, carry):
        cols = pl.ds(pl.multiple_of(m * 128, 128), 128)
        hi, lo = split(crecv[:, cols])
        chl[64:128, cols] = hi
        chl[192:256, cols] = lo
        return carry

    lax.fori_loop(0, 32, sister_rows, 0)
    gather_done(0)
    margins_start(2)
    margins_start(1)
    solve(0)
    scatter_start(0)
    build_operator(40, 64)

    loads[6].wait()
    r_ = lax.broadcasted_iota(jnp.int32, (512, 128), 0)
    q_ = lax.broadcasted_iota(jnp.int32, (512, 128), 1)
    c_, s_ = r_ // 8, r_ % 8
    dx = jnp.where(s_ == 0, 7, jnp.where(s_ == 1, 1, 0))
    dy = jnp.where(s_ == 2, 3, jnp.where(s_ == 3, 1, 0))
    dz = jnp.where(s_ == 4, 3, jnp.where(s_ == 5, 1, 0))
    px = ((c_ // 16) * 2 + core + dx) % 8
    py = ((c_ // 4) % 4 + dy) % 4
    pz = (c_ % 4 + dz) % 4
    wanted = jnp.where(q_ == (px * 4 + py) * 4 + pz, 1.0, 0.0).astype(BF16)
    i_ = lax.broadcasted_iota(jnp.int32, (128, 128), 0)
    ch_ = i_ % 64
    kk_ = (core + i_ // 64) % 2
    block = (((ch_ // 16) * 2 + kk_) * 4 + (ch_ // 4) % 4) * 4 + ch_ % 4
    held = jnp.where(owner_v[...] == block, 1.0, 0.0).astype(BF16)
    sel[...] = dot_nt(wanted, held).astype(BF16)
    swap(0)

    import_margins(2)
    big_product(amat, al0)
    put_pair(xhl, 0, al0[...])
    projected = stacked(bhl[...], xhl[0:OWN, :])

    margins_wait(1)
    basis_t = basis_v[...].T
    hi, lo = split(basis_t)
    bt[0] = hi
    bt[1] = lo
    hi, lo = split(jnp.concatenate([basis_t, jnp.zeros_like(basis_t)], axis=1))
    xg[0:OWN, 0:128] = hi
    xg[0:OWN, 128:256] = lo
    for b in range(6):
        mask = jnp.where((lane_h < 64) == (b % 2 == 0), valid[b], 0.0)
        top, bottom = brecv[b], pltpu.roll(brecv[b], 64, 1)
        if b % 2 == 1:
            top, bottom = bottom, top
        put_pair(xg, OWN + b * OVR, top * mask)
        put_pair(xg, OWN + b * OVR + 128, bottom * mask)

    def coarse_columns(i, carry):
        r = pl.multiple_of(i * 256, 256)
        for j in range(4):
            rows = slice(0, OWN) if j == 3 else slice(OWN + j * 512, OWN + (j + 1) * 512)
            p = dot(amat[0, pl.ds(r, 256), rows], xg[rows, :])
            q = dot(amat[1, pl.ds(r, 256), rows], xg[rows, 0:NRHS])
            hi, lo = split(fold(p, q))
            gmat[0, pl.ds(r, 256), j * 128 : (j + 1) * 128] = hi
            gmat[1, pl.ds(r, 256), j * 128 : (j + 1) * 128] = lo
        return carry

    lax.fori_loop(0, OWN // 256, coarse_columns, 0)
    p = dot(bhl[...], gmat[0])
    h = p[0:K] + p[K:] + dot(bhl[0:K, :], gmat[1])
    hi, lo = split(h)
    hmat[0:K, :] = hi
    hmat[K : 2 * K, :] = lo

    mapped_in(0)

    gat[1, x, y, z] = projected + stacked(hmat[...], mhl[...])
    gather_one(1)
    apply_coarse(al0, w0)
    put_pair(xhl, 0, w0[...])
    outgoing(3)
    gather_two(1)
    margins_start(3)
    dots = totals_start(0, rv, w0)
    add_coarse(l0, u0)
    gather_three(1)
    totals_spread(0, dots)
    import_margins(3)
    big_product(linv, l1)
    put_pair(xhl, 0, l1[...])
    outgoing(4)
    alpha0 = totals_finish(0)
    rv[...] = rv[...] - alpha0 * w0[...]
    first = pltpu.make_async_copy(rv, res_ref, out_sem.at[0])
    first.start()
    gather_done(1)
    margins_start(4)
    solve(1)
    scatter_start(1)
    u0_scaled = alpha0 * u0[...]
    l0[...] = u0_scaled
    second = pltpu.make_async_copy(l0, sol_ref, out_sem.at[1])
    second.start()
    swap(1)
    import_margins(4)
    big_product(amat, al1)
    mapped_in(1)
    apply_coarse(al1, al1)
    w0[...] = w0[...] - alpha0 * al1[...]
    dots = totals_start(1, rv, w0)
    third = pltpu.make_async_copy(w0, image_ref, out_sem.at[2])
    third.start()
    add_coarse(l1, l1)
    l1[...] = u0[...] - alpha0 * l1[...]
    fourth = pltpu.make_async_copy(l1, update_ref, out_sem.at[3])
    totals_spread(1, dots)
    fourth.start()
    alpha_ref[...] = totals_finish(1)

    for copy in pending:
        copy.wait_send()
    scatter_drain(0)
    scatter_drain(1)
    for copy in (first, second, third, fourth):
        copy.wait()


def run(rhs, diagonal, couple, links, exports, linv, basis, cinv, owner):
    field = (OWN, NRHS)
    dma = pltpu.SemaphoreType.DMA
    vm = pltpu.VMEM
    scratch = [
        vm(field, F32),
        vm((K, OWN), F32),
        vm((1, OWN), F32),
        vm((6, 1, OWN), F32),
        vm((6, 1, OWN), jnp.int32),
        vm((6, 1, OVR), jnp.int32),
        vm((1, 128), jnp.int32),
        vm((LSLOTS, LCH, NEXT), F32),
        vm((2, OWN, NEXT), BF16),
        vm((2, OWN, NEXT), BF16),
        vm((6 * OVR, OWN), BF16),
        vm((64, K, 128), F32),
        vm((256, 4096), BF16),
        vm((K, 4096), F32),
        vm((K, 4096), F32),
        vm((2, 4, 4, 4, K, NRHS), F32),
        vm((4096, 256), BF16),
        vm((NEXT, 256), BF16),
        vm((2, 128, OWN), BF16),
        vm((2, OWN, K), BF16),
        vm((128, OWN), BF16),
        vm((4, 6, OVR, NRHS), F32),
        vm((4, 6, OVR, NRHS), F32),
        vm((6, 128, 128), F32),
        vm((6, 128, 128), F32),
        vm(field, F32),
        vm(field, F32),
        vm(field, F32),
        vm(field, F32),
        vm(field, F32),
        vm(field, F32),
        vm((2, OWN, 512), BF16),
        vm((128, 512), BF16),
        vm((512, 128), BF16),
        vm((512, 256), BF16),
        vm((8, OWN), F32),
        vm((8, OWN), F32),
        vm((OVR, 8), F32),
        vm((2, 2, CHIPS, NRHS), F32),
        vm((2, 2, CHIPS, NRHS), F32),
        vm((2, 2, CHIPS, NRHS), F32),
        vm((2, CHIPS, 8, NRHS), F32),
        vm((2, CHIPS, 8, NRHS), F32),
        vm((2, 8, NRHS), F32),
        vm((2, 8, NRHS), F32),
        vm((2, 8, NRHS), F32),
        vm((2, 128, NRHS), F32),
        dma((8,)),
        dma((LSLOTS,)),
        dma((2, 3, 6, 3)),
        dma((2, 3, 6, 3)),
        dma((5, 6)),
        dma((5, 6)),
        dma((2,)),
        dma((2, 6)),
        dma((2, 4)),
        dma((4,)),
    ]
    anywhere = pl.BlockSpec(memory_space=pl.ANY)
    return pl.pallas_call(
        kernel,
        out_shape=[jax.ShapeDtypeStruct(field, F32)] * 4 + [jax.ShapeDtypeStruct((1, NRHS), F32)],
        in_specs=[anywhere] * 8 + [pl.BlockSpec(memory_space=pltpu.SMEM), anywhere],
        out_specs=[anywhere] * 4 + [pl.BlockSpec(memory_space=pltpu.VMEM)],
        scratch_shapes=scratch,
        compiler_params=pltpu.CompilerParams(
            collective_id=0, has_side_effects=True, vmem_limit_bytes=63 * 1024 * 1024
        ),
        cost_estimate=pl.CostEstimate(flops=12_000_000_000, bytes_accessed=15_000_000, transcendentals=0),
    )(rhs, diagonal, couple, links, exports, linv, basis, cinv, owner, owner.reshape(1, 128))


def body(rhs, diagonal, couple, neighbours, export_rows, local_inverse, basis, coarse_inverse, owner):
    first, update, residual, image, alpha = run(
        rhs.reshape(OWN, NRHS),
        diagonal.reshape(1, OWN),
        couple.reshape(6, 1, OWN),
        neighbours.reshape(6, 1, OWN),
        export_rows.reshape(6, 1, OVR),
        local_inverse.reshape(OWN, NEXT),
        basis.reshape(K, OWN),
        coarse_inverse,
        owner,
    )
    return (first + alpha * update).reshape(rhs.shape), (residual - alpha * image).reshape(rhs.shape)


def solution(mesh):
    placed = (
        P("gx", "gy", "gz", None, None),
        P("gx", "gy", "gz", None),
        P("gx", "gy", "gz", None, None),
        P("gx", "gy", "gz", None, None),
        P("gx", "gy", "gz", None, None),
        P("gx", "gy", "gz", None, None),
        P("gx", "gy", "gz", None, None),
        P(("gx", "gy", "gz"), None),
        P(),
    )
    return jax.shard_map(
        body,
        mesh=mesh,
        in_specs=placed,
        out_specs=(P("gx", "gy", "gz", None, None), P("gx", "gy", "gz", None, None)),
        check_vma=False,
    )
```

```python
import jax
import jax.numpy as jnp
from jax import lax
from jax.experimental import pallas as pl
from jax.experimental.pallas import tpu as pltpu
from jax.sharding import PartitionSpec as P

F32 = jnp.float32
BF16 = jnp.bfloat16
MESH = pl.DeviceIdType.MESH

OWN = 1024
NRHS = 128
K = 64
OVR = 256
NEXT = 2560
CHIPS = 64
LCH = 128
NLCH = OWN // LCH
LSLOTS = 4

SHARES = ((0, 24, (2, 1, 0)), (24, 24, (0, 2, 1)), (48, 16, (1, 0, 2)))


A1, A2, A3, A4 = 0, 0, 6, 10


def split(x):
    hi = x.astype(BF16)
    lo = (x - hi.astype(F32)).astype(BF16)
    return hi, lo


def put_pair(ref, start, x):
    hi, lo = split(x)
    rows = x.shape[0]
    ref[pl.ds(start, rows), 0:NRHS] = hi
    ref[pl.ds(start, rows), NRHS : 2 * NRHS] = lo


def dot(a, b):
    return jnp.dot(a, b, preferred_element_type=F32)


def dot_nt(a, b):
    return lax.dot_general(a, b, (((1,), (1,)), ((), ())), preferred_element_type=F32)


def fold(p, q):
    return p[:, 0:NRHS] + p[:, NRHS : 2 * NRHS] + q


def stacked(s, x):
    p = dot(s, x)
    half = s.shape[0] // 2
    return fold(p[0:half], p[half:, 0:NRHS])


def ring(v, n):
    return [v] + [lax.rem(v + d, n) for d in range(1, n)]


def hops(d):
    return sum((0, 1, 2, 1)[i] for i in (d // 16, (d // 4) % 4, d % 4))


def kernel(
    rhs_h,
    diag_h,
    couple_h,
    links_h,
    exports_h,
    linv_h,
    basis_h,
    cinv_h,
    owner_s,
    owner_h,
    sol_ref,
    update_ref,
    res_ref,
    image_ref,
    alpha_ref,
    rv,
    basis_v,
    diag_v,
    couple_v,
    links_v,
    exports_v,
    owner_v,
    lstage,
    linv,
    amat,
    emat,
    cinv_v,
    chl,
    csend,
    crecv,
    gat,
    xg,
    xhl,
    bcat,
    bt,
    bhl,
    msend,
    mrecv,
    bsend,
    brecv,
    l0,
    u0,
    w0,
    l1,
    al1,
    gmat,
    hmat,
    sel,
    mhl,
    tcol,
    ncol,
    wrow,
    trow,
    bamat,
    rmat,
    ecol,
    psrc,
    rbuf,
    sbuf,
    ssend,
    srecv,
    dsend,
    dsis,
    dpair,
    dall,
    in_sem,
    l_sem,
    g_ss,
    g_rs,
    m_ss,
    m_rs,
    c_sem,
    s_sem,
    d_sem,
    out_sem,
):
    gx = lax.axis_index("gx")
    y = lax.axis_index("gy")
    z = lax.axis_index("gz")
    x, core = gx // 2, lax.rem(gx, 2)
    chip = (x * 4 + y) * 4 + z
    RX, RY, RZ = ring(x, 4), ring(y, 4), ring(z, 4)
    sister = (x * 2 + 1 - core, y, z)
    place = [x, y, z]

    def at(a, b, c):
        return (a * 2 + core, b, c)

    def along(axis, d):
        p = list(place)
        p[axis] = (RX, RY, RZ)[axis][d]
        return at(*p)

    pending = []

    def send(src, dst, ssem, rsem, device):
        copy = pltpu.make_async_remote_copy(
            src_ref=src, dst_ref=dst, send_sem=ssem, recv_sem=rsem, device_id=device, device_id_type=MESH
        )
        copy.start()
        pending.append(copy)
        return copy

    loads = []
    for i, (src, dst) in enumerate(
        (
            (basis_h, basis_v),
            (rhs_h, rv),
            (exports_h, exports_v),
            (couple_h, couple_v),
            (links_h, links_v),
            (diag_h, diag_v),
            (owner_h, owner_v),
        )
    ):
        copy = pltpu.make_async_copy(src, dst, in_sem.at[i])
        copy.start()
        loads.append(copy)

    def load_columns(t):
        return pltpu.make_async_copy(cinv_h.at[:, pl.ds(pl.multiple_of(t * 128, 128), 128)], cinv_v.at[t], in_sem.at[7])

    def load_column(t, carry):
        load_columns(t).start()
        return carry

    lax.fori_loop(0, 64, load_column, 0)

    def load_chunk(c):
        return pltpu.make_async_copy(linv_h.at[pl.ds(c * LCH, LCH)], lstage.at[c % LSLOTS], l_sem.at[c % LSLOTS])

    for c in range(LSLOTS):
        load_chunk(c).start()

    far = []
    for d in sorted(range(1, CHIPS), key=hops, reverse=True):
        a, b, c = RX[d // 16], RY[(d // 4) % 4], RZ[d % 4]
        far.append(((a * 4 + b) * 4 + c, at(a, b, c)))
    gx_up = (lax.rem(gx + 1, 8), y, z)
    gx_down = (lax.rem(gx + 7, 8), y, z)
    across = (lax.rem(gx + 7 + 2 * core, 8), y, z)
    bar = pltpu.get_barrier_semaphore()
    near = [along(axis, d) for d in (2, 1, 3) for axis in range(3)] + [across, sister]
    for device in near:
        pl.semaphore_signal(bar, inc=1, device_id=device, device_id_type=MESH)

    def region(n, t, stage, line=0):
        start, rows, order = SHARES[t]
        index = [slice(None) if a in order[:stage] else place[a] for a in range(3)]
        if stage == 2:
            axis = order[1]
            index[axis] = (RX, RY, RZ)[axis][line]
        return gat.at[n].at[index[0], index[1], index[2], pl.ds(start, rows), :]

    def gather_send(n, stage, line=0):
        slot = stage + line
        for t in range(3):
            reg = region(n, t, stage, line)
            for j, d in enumerate((1, 3, 2)):
                send(reg, reg, g_ss.at[n, t, slot, j], g_rs.at[n, t, slot, j], along(SHARES[t][2][stage], d))

    def gather_recv(n, stage, line=0):
        for t in range(3):
            reg = region(n, t, stage, line)
            for j in range(3):
                pltpu.make_async_copy(reg, reg, g_rs.at[n, t, stage + line, j]).wait()

    def gather_one(n):
        gather_send(n, 0)

    def gather_two(n):
        gather_recv(n, 0)
        gather_send(n, 1)
        gather_send(n, 2, 0)

    def gather_three(n):
        gather_recv(n, 1)
        for line in (1, 3, 2):
            gather_send(n, 2, line)

    def gather_done(n):
        for line in (0, 1, 3, 2):
            gather_recv(n, 2, line)

    steps = (
        (gx_up, gx_down),
        ((gx, RY[1], z), (gx, RY[3], z)),
        ((gx, y, RZ[1]), (gx, y, RZ[3])),
    )
    valid = []
    for coordinate, length in ((gx, 8), (y, 4), (z, 4)):
        valid.append(jnp.where(coordinate > 0, 1.0, 0.0).astype(F32))
        valid.append(jnp.where(coordinate < length - 1, 1.0, 0.0).astype(F32))

    def margins(n):
        return (bsend, brecv) if n == 1 else (msend.at[n if n == 0 else n - 1], mrecv.at[n if n == 0 else n - 1])

    def margins_start(n):
        out, into = margins(n)
        for e in range(3):
            up, down = steps[e]
            send(out.at[2 * e + 1], into.at[2 * e], m_ss.at[n, 2 * e], m_rs.at[n, 2 * e], up)
            send(out.at[2 * e], into.at[2 * e + 1], m_ss.at[n, 2 * e + 1], m_rs.at[n, 2 * e + 1], down)

    def margins_wait(n):
        into = margins(n)[1]
        for b in range(6):
            pltpu.make_async_copy(into.at[b], into.at[b], m_rs.at[n, b]).wait()

    def outgoing(n):
        out = margins(n)[0]

        for d in range(0, 6, 2):
            p = dot(emat[d * OVR : (d + 2) * OVR, :], xhl[0:OWN, :])
            q = p[:, 0:NRHS] + p[:, NRHS:]
            out[d] = q[0:OVR]
            out[d + 1] = q[OVR:]

    def import_margins(n):
        margins_wait(n)
        into = margins(n)[1]
        for b in range(6):
            put_pair(xhl, OWN + b * OVR, into[b] * valid[b])

    def product_owned(mat, dst):
        def step(i, carry):
            r = pl.multiple_of(i * 512, 512)
            p = dot(mat[0, pl.ds(r, 512), 0:OWN], xhl[0:OWN, :])
            q = dot(mat[1, pl.ds(r, 512), 0:OWN], xhl[0:OWN, 0:NRHS])
            dst[pl.ds(r, 512), :] = fold(p, q)
            return carry

        lax.fori_loop(0, OWN // 512, step, 0)

    def product_margins(mat, dst):
        def step(i, carry):
            r = pl.multiple_of(i * 512, 512)
            p = dot(mat[0, pl.ds(r, 512), OWN:], xhl[OWN:, :])
            q = dot(mat[1, pl.ds(r, 512), OWN:], xhl[OWN:, 0:NRHS])
            dst[pl.ds(r, 512), :] = dst[pl.ds(r, 512), :] + fold(p, q)
            return carry

        lax.fori_loop(0, OWN // 512, step, 0)

    def solve(n):
        total = jnp.zeros((256, 256), F32)
        for a in range(4):
            for b in range(4):
                put_pair(xg, (a * 4 + b) * 256, gat[n, a, b].reshape(256, NRHS))
            total = total + dot(chl[:, a * 1024 : (a + 1) * 1024], xg[a * 1024 : (a + 1) * 1024, :])
        res = total[0:128, 0:NRHS] + total[0:128, NRHS:] + total[128:256, 0:NRHS]
        psrc[n, 0] = res[0:64]
        psrc[n, 1] = res[64:128]

    def scatter_start(n):
        for c, device in far:
            copy = pltpu.make_async_remote_copy(
                src_ref=psrc.at[n, :, c, :],
                dst_ref=rbuf.at[n, :, chip, :],
                send_sem=s_sem.at[n, 0],
                recv_sem=s_sem.at[n, 1],
                device_id=device,
                device_id_type=MESH,
            )
            copy.start()
        rbuf[n, :, pl.ds(chip, 1), :] = psrc[n, :, pl.ds(chip, 1), :]

    def wait_all(ref, sem):
        pltpu.make_async_copy(ref, ref, sem).wait()

    def swap(n):
        wait_all(rbuf.at[n, :, pl.ds(0, 63), :], s_sem.at[n, 1])
        send(rbuf.at[n], sbuf.at[n], s_sem.at[n, 2], s_sem.at[n, 3], sister).wait_recv()
        first = rbuf[n, 0] + sbuf[n, 1]
        second = rbuf[n, 1] + sbuf[n, 0]
        hi, lo = split(jnp.concatenate([first, second], axis=0))
        p = dot(sel[...], jnp.concatenate([hi, lo], axis=1))
        ssend[n] = (p[:, 0:NRHS] + p[:, NRHS:]).reshape(CHIPS, 8, NRHS)
        for c, device in far:
            copy = pltpu.make_async_remote_copy(
                src_ref=ssend.at[n, c, pl.ds(0, 7)],
                dst_ref=srecv.at[n, chip, pl.ds(0, 7)],
                send_sem=s_sem.at[n, 4],
                recv_sem=s_sem.at[n, 5],
                device_id=device,
                device_id_type=MESH,
            )
            copy.start()
        srecv[n, chip, 0:7] = ssend[n, chip, 0:7]

    def mapped_in(n):
        wait_all(srecv.at[n, pl.ds(0, 63), pl.ds(0, 7)], s_sem.at[n, 5])
        for s in range(7):
            put_pair(mhl, s * K, srecv[n, :, s, :])

    def scatter_drain(n):
        wait_all(rbuf.at[n, :, pl.ds(0, 63), :], s_sem.at[n, 0])
        wait_all(srecv.at[n, pl.ds(0, 63), pl.ds(0, 7)], s_sem.at[n, 4])

    def add_coarse(base, dst):
        mine = mhl[6 * K : 7 * K, :]
        dst[...] = base[...] + fold(dot(bt[0], mine), dot(bt[1], mine[:, 0:NRHS]))

    def apply_coarse(base, dst):
        def step(i, carry):
            r = pl.multiple_of(i * 256, 256)
            p = dot(gmat[0, pl.ds(r, 256), :], mhl[...])
            q = dot(gmat[1, pl.ds(r, 256), :], mhl[:, 0:NRHS])
            dst[pl.ds(r, 256), :] = base[pl.ds(r, 256), :] + fold(p, q)
            return carry

        lax.fori_loop(0, OWN // 256, step, 0)

    def totals_start(n, left, right):
        dsend[n] = jnp.zeros((8, NRHS), F32)
        dsend[n, 0:1, :] = jnp.sum(left[...] * right[...], axis=0, keepdims=True)
        dsend[n, 1:2, :] = jnp.sum(right[...] * right[...], axis=0, keepdims=True)
        return send(dsend.at[n], dsis.at[n], d_sem.at[n, 0], d_sem.at[n, 1], sister)

    def totals_spread(n, copy):
        copy.wait_recv()
        dpair[n] = dsend[n] + dsis[n]
        for c, device in far:
            copy = pltpu.make_async_remote_copy(
                src_ref=dpair.at[n, pl.ds(0, 2)],
                dst_ref=dall.at[n, pl.ds(2 * chip, 2)],
                send_sem=d_sem.at[n, 2],
                recv_sem=d_sem.at[n, 3],
                device_id=device,
                device_id_type=MESH,
            )
            copy.start()
        dall[n, pl.ds(2 * chip, 2)] = dpair[n, 0:2]

    def totals_finish(n):
        wait_all(dall.at[n, pl.ds(0, 126)], d_sem.at[n, 3])
        cross = jnp.sum(dall[n, pl.ds(0, 64, stride=2), :], axis=0, keepdims=True)
        energy = jnp.sum(dall[n, pl.ds(1, 64, stride=2), :], axis=0, keepdims=True)
        wait_all(dall.at[n, pl.ds(0, 126)], d_sem.at[n, 2])
        return cross / energy

    mhl[7 * K :, :] = jnp.zeros((K, 2 * NRHS), BF16)
    loads[0].wait()
    loads[1].wait()
    put_pair(xhl, 0, rv[...])
    hi, lo = split(basis_v[...])
    bhl[0:K, :] = hi
    bhl[K : 2 * K, :] = lo
    gat[0, x, y, z] = stacked(bhl[...], xhl[0:OWN, :])

    loads[2].wait()
    tcol[...] = jnp.zeros_like(tcol)
    ncol[...] = jnp.zeros_like(ncol)
    for d in range(6):
        tcol[d : d + 1, 0:OVR] = exports_v[d].astype(F32)
    ecol[...] = tcol[...][:, 0:OVR].T

    def export_rows(g, carry):
        r = pl.multiple_of(g * 16, 16)
        rows = ecol[pl.ds(r, 16), :]
        lanes = lax.broadcasted_iota(jnp.int32, (16, 128), 1)
        one, zero = jnp.ones((16, 128), BF16), jnp.zeros((16, 128), BF16)
        for d in range(6):
            place_d = jnp.broadcast_to(rows[:, d : d + 1], (16, 128)).astype(jnp.int32).astype(jnp.int16)
            for j in range(OWN // 128):
                hit = (lanes + j * 128).astype(jnp.int16) == place_d
                emat[pl.ds(d * OVR + r, 16), j * 128 : (j + 1) * 128] = jnp.where(hit, one, zero)
        return carry

    pltpu.make_async_copy(cinv_v, cinv_v, in_sem.at[7]).wait()
    lane = lax.broadcasted_iota(jnp.int32, (K, 128), 1)

    def column_block(c, kk, half):
        cx, cy, cz = c // 16, lax.rem(c // 4, 4), lax.rem(c, 4)
        j = owner_s[((cx * 2 + kk) * 4 + cy) * 4 + cz]
        pair = lax.shift_right_logical(j, 1)
        tile = cinv_v[pair]
        turned = pltpu.roll(tile, 64, 1)
        same = jnp.full((K, 128), j - 2 * pair, jnp.int32) == half
        return jnp.where(same, tile, turned)

    def column_pair(m, kk):
        return jnp.where(lane < 64, column_block(2 * m, kk, 0), column_block(2 * m + 1, kk, 1))

    def order_other(i, carry):
        for m in range(4):
            m = 4 * i + m
            csend[:, pl.ds(pl.multiple_of(m * 128, 128), 128)] = column_pair(m, 1 - core)
        return carry

    def order_mine(i, carry):
        for m in range(4):
            m = 4 * i + m
            hi, lo = split(column_pair(m, core))
            chl[0:64, pl.ds(pl.multiple_of(m * 128, 128), 128)] = hi
            chl[128:192, pl.ds(pl.multiple_of(m * 128, 128), 128)] = lo
        return carry

    lax.fori_loop(0, 8, order_other, 0)

    for i in (3, 4, 5):
        loads[i].wait()
    own_row = lax.broadcasted_iota(jnp.int32, (1, OWN), 1)
    targets = [links_v[k] for k in range(6)]
    weights = [couple_v[k] for k in range(6)]
    centre = diag_v[...] + 6.0
    for k in range(6):
        centre = centre - jnp.where(targets[k] == own_row, weights[k], 0.0)
        gone = targets[k] == own_row
        total = weights[k]
        for m in range(6):
            if m < k:
                gone = gone | (targets[m] == targets[k])
            if m > k:
                total = total + jnp.where(targets[m] == targets[k], weights[m], 0.0)
        tcol[k : k + 1, :] = -total
        ncol[k : k + 1, :] = jnp.where(gone, -1, targets[k]).astype(F32)
    tcol[6:7, :] = centre
    ncol[6:7, :] = own_row.astype(F32)
    tcol[7:8, :] = jnp.zeros((1, OWN), F32)
    ncol[7:8, :] = jnp.full((1, OWN), -1.0, F32)

    def by_groups(ref, into):
        row = lax.broadcasted_iota(jnp.int32, (8, 128), 0)
        part = lax.broadcasted_iota(jnp.int32, (8, 128), 1) // 16
        for c in range(8):
            block = ref[:, c * 128 : (c + 1) * 128]
            turned = jnp.zeros((8, 128), F32)
            for d in range(8):
                moved = block if d == 0 else pltpu.roll(pltpu.roll(block, 8 - d, 0), 16 * d, 1)
                turned = jnp.where((part - row + 8) % 8 == d, moved, turned)
            into[c * 8 : (c + 1) * 8, :] = turned

    by_groups(tcol, wrow)
    by_groups(ncol, trow)

    def operator_rows(i, carry):
        lanes = lax.broadcasted_iota(jnp.int32, (16, 128), 1)
        row = lax.broadcasted_iota(jnp.int32, (16, 128), 0)
        cell = lanes % 16 == row
        one, zero = jnp.ones((16, 128), BF16), jnp.zeros((16, 128), BF16)
        for g in range(4):
            g = 4 * i + g
            w = jnp.broadcast_to(wrow[pl.ds(g, 1), :], (16, 128))
            t = jnp.broadcast_to(trow[pl.ds(g, 1), :], (16, 128)).astype(jnp.int32)
            high = lax.shift_right_arithmetic(t, 8)
            low = (t - high * 256).astype(F32).astype(BF16)
            whi, wlo = split(jnp.where(cell, w, 0.0))
            tile = jnp.where(cell, high, -1).astype(F32).astype(BF16)
            his, los = [], []
            for j in range(NEXT // 256):
                hit = tile == jnp.asarray(j, BF16)
                his.append(jnp.where(hit, whi, zero))
                los.append(jnp.where(hit, wlo, zero))
            spots = [jnp.where((row + 16 * q).astype(F32).astype(BF16) == low, one, zero) for q in range(16)]
            placed = dot_nt(jnp.concatenate(his + los, axis=0), jnp.concatenate(spots, axis=0)).astype(BF16)
            r = pl.multiple_of(g * 16, 16)
            for j in range(NEXT // 256):
                amat[0, pl.ds(r, 16), j * 256 : (j + 1) * 256] = placed[16 * j : 16 * j + 16]
                amat[1, pl.ds(r, 16), j * 256 : (j + 1) * 256] = placed[160 + 16 * j : 176 + 16 * j]
        return carry

    def build_operator(first, last):
        lax.fori_loop(first, last, operator_rows, 0)

    build_operator(0, A1)
    pl.semaphore_wait(bar, len(near))
    gather_one(0)
    ccopy = send(csend, crecv, c_sem.at[0], c_sem.at[1], sister)
    lax.fori_loop(0, OVR // 16, export_rows, 0)
    outgoing(0)
    margins_start(0)
    build_operator(A1, A2)
    gather_two(0)
    lax.fori_loop(0, 8, order_mine, 0)
    build_operator(A2, A3)
    gather_three(0)

    for c in range(NLCH):
        load_chunk(c).wait()

        def halves(g, carry):
            r = pl.multiple_of(g * 16, 16)
            hi, lo = split(lstage[c % LSLOTS, pl.ds(r, 16), :])
            linv[0, pl.ds(c * LCH + r, 16), :] = hi
            linv[1, pl.ds(c * LCH + r, 16), :] = lo
            return carry

        lax.fori_loop(0, LCH // 16, halves, 0)
        if c + LSLOTS < NLCH:
            load_chunk(c + LSLOTS).start()

    product_owned(linv, l0)
    import_margins(0)
    product_margins(linv, l0)
    put_pair(xhl, 0, l0[...])
    outgoing(2)
    build_operator(A3, A4)

    basis_t = basis_v[...].T
    hi, lo = split(basis_t)
    bt[0] = hi
    bt[1] = lo
    bcat[...] = jnp.concatenate([hi, hi, lo, lo], axis=1)
    lane_h = lax.broadcasted_iota(jnp.int32, (128, 128), 1)
    for d in range(0, 6, 2):
        p = dot(emat[d * OVR : (d + 2) * OVR, :], bcat[...])
        q = p[:, 0:NRHS] + p[:, NRHS:]
        bsend[d] = jnp.where(lane_h < 64, q[0:128], q[128:256])
        bsend[d + 1] = jnp.where(lane_h < 64, q[256:384], q[384:512])

    ccopy.wait_recv()

    def sister_rows(m, carry):
        cols = pl.ds(pl.multiple_of(m * 512, 512), 512)
        hi, lo = split(crecv[:, cols])
        chl[64:128, cols] = hi
        chl[192:256, cols] = lo
        return carry

    lax.fori_loop(0, 8, sister_rows, 0)
    gather_done(0)
    margins_start(2)
    margins_start(1)
    solve(0)
    scatter_start(0)
    build_operator(A4, 16)

    loads[6].wait()
    r_ = lax.broadcasted_iota(jnp.int32, (512, 128), 0)
    q_ = lax.broadcasted_iota(jnp.int32, (512, 128), 1)
    c_, s_ = r_ // 8, r_ % 8
    dx = jnp.where(s_ == 0, 7, jnp.where(s_ == 1, 1, 0))
    dy = jnp.where(s_ == 2, 3, jnp.where(s_ == 3, 1, 0))
    dz = jnp.where(s_ == 4, 3, jnp.where(s_ == 5, 1, 0))
    px = ((c_ // 16) * 2 + core + dx) % 8
    py = ((c_ // 4) % 4 + dy) % 4
    pz = (c_ % 4 + dz) % 4
    wanted = jnp.where(q_ == (px * 4 + py) * 4 + pz, 1.0, 0.0).astype(BF16)
    i_ = lax.broadcasted_iota(jnp.int32, (128, 128), 0)
    ch_ = i_ % 64
    kk_ = (core + i_ // 64) % 2
    block = (((ch_ // 16) * 2 + kk_) * 4 + (ch_ // 4) % 4) * 4 + ch_ % 4
    held = jnp.where(owner_v[...] == block, 1.0, 0.0).astype(BF16)
    sel[...] = dot_nt(wanted, held).astype(BF16)
    for j in range(0, NEXT, 512):
        p = dot(bhl[...], amat[0, :, j : j + 512])
        hi, lo = split(p[0:K] + p[K:] + dot(bhl[0:K, :], amat[1, :, j : j + 512]))
        bamat[0:K, j : j + 512] = hi
        bamat[K:, j : j + 512] = lo
    swap(0)

    margins_wait(1)
    hi, lo = split(jnp.concatenate([basis_t, jnp.zeros_like(basis_t)], axis=1))
    rmat[0:OWN, 0:128] = hi
    rmat[0:OWN, 128:256] = lo
    for b in range(6):
        mask = jnp.where((lane_h < 64) == (b % 2 == 0), valid[b], 0.0)
        top, bottom = brecv[b], pltpu.roll(brecv[b], 64, 1)
        if b % 2 == 1:
            top, bottom = bottom, top
        put_pair(rmat, OWN + b * OVR, top * mask)
        put_pair(rmat, OWN + b * OVR + 128, bottom * mask)
    spans = [(OWN + j * 512, OWN + (j + 1) * 512) for j in range(3)] + [(0, OWN)]
    for j, (start, stop) in enumerate(spans):
        hi, lo = split(stacked(bamat[:, start:stop], rmat[start:stop, :]))
        hmat[0:K, j * 128 : (j + 1) * 128] = hi
        hmat[K:, j * 128 : (j + 1) * 128] = lo
    import_margins(2)
    projected = stacked(bamat[...], xhl[...])
    mapped_in(0)

    gat[1, x, y, z] = projected + stacked(hmat[...], mhl[...])
    gather_one(1)
    add_coarse(l0, u0)
    put_pair(xhl, 0, u0[...])
    into = margins(2)[1]
    for j in range(3):
        start, stop = spans[j]
        part = mhl[j * 128 : (j + 1) * 128, :]
        more = fold(dot(rmat[start:stop, 0:NRHS], part), dot(rmat[start:stop, NRHS:], part[:, 0:NRHS]))
        put_pair(xhl, start, into[2 * j] * valid[2 * j] + more[0:OVR])
        put_pair(xhl, start + OVR, into[2 * j + 1] * valid[2 * j + 1] + more[OVR:])
    product_owned(amat, w0)
    product_margins(amat, w0)
    put_pair(xhl, 0, w0[...])
    outgoing(3)
    gather_two(1)
    margins_start(3)
    dots = totals_start(0, rv, w0)
    product_owned(linv, l1)
    gather_three(1)
    totals_spread(0, dots)
    import_margins(3)
    product_margins(linv, l1)
    put_pair(xhl, 0, l1[...])
    outgoing(4)
    margins_start(4)
    alpha0 = totals_finish(0)
    rv[...] = rv[...] - alpha0 * w0[...]
    first = pltpu.make_async_copy(rv, res_ref, out_sem.at[0])
    first.start()
    gather_done(1)
    solve(1)
    scatter_start(1)
    u0_scaled = alpha0 * u0[...]
    l0[...] = u0_scaled
    second = pltpu.make_async_copy(l0, sol_ref, out_sem.at[1])
    second.start()
    product_owned(amat, al1)
    swap(1)
    import_margins(4)
    product_margins(amat, al1)

    def coarse_columns(i, carry):
        r = pl.multiple_of(i * 512, 512)
        for j, (start, stop) in enumerate(spans):
            p = dot(amat[0, pl.ds(r, 512), start:stop], rmat[start:stop, :])
            q = dot(amat[1, pl.ds(r, 512), start:stop], rmat[start:stop, 0:NRHS])
            hi, lo = split(fold(p, q))
            gmat[0, pl.ds(r, 512), j * 128 : (j + 1) * 128] = hi
            gmat[1, pl.ds(r, 512), j * 128 : (j + 1) * 128] = lo
        return carry

    lax.fori_loop(0, OWN // 512, coarse_columns, 0)
    mapped_in(1)
    apply_coarse(al1, al1)
    w0[...] = w0[...] - alpha0 * al1[...]
    dots = totals_start(1, rv, w0)
    third = pltpu.make_async_copy(w0, image_ref, out_sem.at[2])
    third.start()
    add_coarse(l1, l1)
    l1[...] = u0[...] - alpha0 * l1[...]
    fourth = pltpu.make_async_copy(l1, update_ref, out_sem.at[3])
    totals_spread(1, dots)
    fourth.start()
    alpha_ref[...] = totals_finish(1)

    for copy in pending:
        copy.wait_send()
    scatter_drain(0)
    scatter_drain(1)
    for copy in (first, second, third, fourth):
        copy.wait()


def run(rhs, diagonal, couple, links, exports, linv, basis, cinv, owner):
    field = (OWN, NRHS)
    dma = pltpu.SemaphoreType.DMA
    vm = pltpu.VMEM
    scratch = [
        vm(field, F32),
        vm((K, OWN), F32),
        vm((1, OWN), F32),
        vm((6, 1, OWN), F32),
        vm((6, 1, OWN), jnp.int32),
        vm((6, 1, OVR), jnp.int32),
        vm((1, 128), jnp.int32),
        vm((LSLOTS, LCH, NEXT), F32),
        vm((2, OWN, NEXT), BF16),
        vm((2, OWN, NEXT), BF16),
        vm((6 * OVR, OWN), BF16),
        vm((64, K, 128), F32),
        vm((256, 4096), BF16),
        vm((K, 4096), F32),
        vm((K, 4096), F32),
        vm((2, 4, 4, 4, K, NRHS), F32),
        vm((4096, 256), BF16),
        vm((NEXT, 256), BF16),
        vm((OWN, 256), BF16),
        vm((2, OWN, K), BF16),
        vm((128, OWN), BF16),
        vm((4, 6, OVR, NRHS), F32),
        vm((4, 6, OVR, NRHS), F32),
        vm((6, 128, 128), F32),
        vm((6, 128, 128), F32),
        vm(field, F32),
        vm(field, F32),
        vm(field, F32),
        vm(field, F32),
        vm(field, F32),
        vm((2, OWN, 512), BF16),
        vm((128, 512), BF16),
        vm((512, 128), BF16),
        vm((512, 256), BF16),
        vm((8, OWN), F32),
        vm((8, OWN), F32),
        vm((64, 128), F32),
        vm((64, 128), F32),
        vm((128, NEXT), BF16),
        vm((NEXT, 256), BF16),
        vm((OVR, 8), F32),
        vm((2, 2, CHIPS, NRHS), F32),
        vm((2, 2, CHIPS, NRHS), F32),
        vm((2, 2, CHIPS, NRHS), F32),
        vm((2, CHIPS, 8, NRHS), F32),
        vm((2, CHIPS, 8, NRHS), F32),
        vm((2, 8, NRHS), F32),
        vm((2, 8, NRHS), F32),
        vm((2, 8, NRHS), F32),
        vm((2, 128, NRHS), F32),
        dma((8,)),
        dma((LSLOTS,)),
        dma((2, 3, 6, 3)),
        dma((2, 3, 6, 3)),
        dma((5, 6)),
        dma((5, 6)),
        dma((2,)),
        dma((2, 6)),
        dma((2, 4)),
        dma((4,)),
    ]
    anywhere = pl.BlockSpec(memory_space=pl.ANY)
    return pl.pallas_call(
        kernel,
        out_shape=[jax.ShapeDtypeStruct(field, F32)] * 4 + [jax.ShapeDtypeStruct((1, NRHS), F32)],
        in_specs=[anywhere] * 8 + [pl.BlockSpec(memory_space=pltpu.SMEM), anywhere],
        out_specs=[anywhere] * 4 + [pl.BlockSpec(memory_space=pltpu.VMEM)],
        scratch_shapes=scratch,
        compiler_params=pltpu.CompilerParams(
            collective_id=0, has_side_effects=True, vmem_limit_bytes=63 * 1024 * 1024
        ),
        cost_estimate=pl.CostEstimate(flops=12_000_000_000, bytes_accessed=15_000_000, transcendentals=0),
    )(rhs, diagonal, couple, links, exports, linv, basis, cinv, owner, owner.reshape(1, 128))


def body(rhs, diagonal, couple, neighbours, export_rows, local_inverse, basis, coarse_inverse, owner):
    first, update, residual, image, alpha = run(
        rhs.reshape(OWN, NRHS),
        diagonal.reshape(1, OWN),
        couple.reshape(6, 1, OWN),
        neighbours.reshape(6, 1, OWN),
        export_rows.reshape(6, 1, OVR),
        local_inverse.reshape(OWN, NEXT),
        basis.reshape(K, OWN),
        coarse_inverse,
        owner,
    )
    return (first + alpha * update).reshape(rhs.shape), (residual - alpha * image).reshape(rhs.shape)


def solution(mesh):
    placed = (
        P("gx", "gy", "gz", None, None),
        P("gx", "gy", "gz", None),
        P("gx", "gy", "gz", None, None),
        P("gx", "gy", "gz", None, None),
        P("gx", "gy", "gz", None, None),
        P("gx", "gy", "gz", None, None),
        P("gx", "gy", "gz", None, None),
        P(("gx", "gy", "gz"), None),
        P(),
    )
    return jax.shard_map(
        body,
        mesh=mesh,
        in_specs=placed,
        out_specs=(P("gx", "gy", "gz", None, None), P("gx", "gy", "gz", None, None)),
        check_vma=False,
    )
```

```python
import jax
import jax.numpy as jnp
from jax import lax
from jax.experimental import pallas as pl
from jax.experimental.pallas import tpu as pltpu
from jax.sharding import PartitionSpec as P

F32 = jnp.float32
BF16 = jnp.bfloat16
MESH = pl.DeviceIdType.MESH

OWN = 1024
NRHS = 128
K = 64
OVR = 256
NEXT = 2560
CHIPS = 64
LCH = 128
NLCH = OWN // LCH
LSLOTS = 4

SHARES = ((0, 22, (2, 1, 0)), (22, 21, (0, 2, 1)), (43, 21, (1, 0, 2)))


A1, A2 = 2, 3


def split(x):
    hi = x.astype(BF16)
    lo = (x - hi.astype(F32)).astype(BF16)
    return hi, lo


def put_pair(ref, start, x):
    hi, lo = split(x)
    rows = x.shape[0]
    ref[pl.ds(start, rows), 0:NRHS] = hi
    ref[pl.ds(start, rows), NRHS : 2 * NRHS] = lo


def dot(a, b):
    return jnp.dot(a, b, preferred_element_type=F32)


def dot_nt(a, b):
    return lax.dot_general(a, b, (((1,), (1,)), ((), ())), preferred_element_type=F32)


def fold(p, q):
    return p[:, 0:NRHS] + p[:, NRHS : 2 * NRHS] + q


def stacked(s, x):
    p = dot(s, x)
    half = s.shape[0] // 2
    return fold(p[0:half], p[half:, 0:NRHS])


def ring(v, n):
    return [v] + [lax.rem(v + d, n) for d in range(1, n)]


def hops(d):
    return sum((0, 1, 2, 1)[i] for i in (d // 16, (d // 4) % 4, d % 4))


def kernel(
    rhs_h,
    diag_h,
    couple_h,
    links_h,
    exports_h,
    linv_h,
    basis_h,
    cinv_h,
    owner_s,
    owner_h,
    sol_ref,
    update_ref,
    res_ref,
    image_ref,
    alpha_ref,
    rv,
    basis_v,
    diag_v,
    couple_v,
    links_v,
    exports_v,
    owner_v,
    lstage,
    linv,
    amat,
    emat,
    cinv_v,
    chl,
    csend,
    crecv,
    gat,
    xg,
    xhl,
    bcat,
    bt,
    bhl,
    msend,
    mrecv,
    bsend,
    brecv,
    l0,
    u0,
    w0,
    l1,
    al1,
    gmat,
    hmat,
    sel,
    mhl,
    tcol,
    ncol,
    wrow,
    trow,
    bamat,
    rmat,
    ecol,
    psrc,
    rbuf,
    sbuf,
    ssend,
    srecv,
    dsend,
    dsis,
    dpair,
    dall,
    in_sem,
    l_sem,
    g_ss,
    g_rs,
    m_ss,
    m_rs,
    c_sem,
    s_sem,
    d_sem,
    out_sem,
):
    gx = lax.axis_index("gx")
    y = lax.axis_index("gy")
    z = lax.axis_index("gz")
    x, core = gx // 2, lax.rem(gx, 2)
    chip = (x * 4 + y) * 4 + z
    RX, RY, RZ = ring(x, 4), ring(y, 4), ring(z, 4)
    sister = (x * 2 + 1 - core, y, z)
    place = [x, y, z]

    def at(a, b, c):
        return (a * 2 + core, b, c)

    def along(axis, d):
        p = list(place)
        p[axis] = (RX, RY, RZ)[axis][d]
        return at(*p)

    pending = []

    def send(src, dst, ssem, rsem, device):
        copy = pltpu.make_async_remote_copy(
            src_ref=src, dst_ref=dst, send_sem=ssem, recv_sem=rsem, device_id=device, device_id_type=MESH
        )
        copy.start()
        pending.append(copy)
        return copy

    loads = []
    for i, (src, dst) in enumerate(
        (
            (basis_h, basis_v),
            (rhs_h, rv),
            (exports_h, exports_v),
            (couple_h, couple_v),
            (links_h, links_v),
            (diag_h, diag_v),
            (owner_h, owner_v),
        )
    ):
        copy = pltpu.make_async_copy(src, dst, in_sem.at[i])
        copy.start()
        loads.append(copy)

    def load_columns(t):
        return pltpu.make_async_copy(cinv_h.at[:, pl.ds(pl.multiple_of(t * 128, 128), 128)], cinv_v.at[t], in_sem.at[7])

    def load_column(t, carry):
        load_columns(t).start()
        return carry

    lax.fori_loop(0, 64, load_column, 0)

    def load_chunk(c):
        return pltpu.make_async_copy(linv_h.at[pl.ds(c * LCH, LCH)], lstage.at[c % LSLOTS], l_sem.at[c % LSLOTS])

    for c in range(LSLOTS):
        load_chunk(c).start()

    far = []
    for d in sorted(range(1, CHIPS), key=hops, reverse=True):
        a, b, c = RX[d // 16], RY[(d // 4) % 4], RZ[d % 4]
        far.append(((a * 4 + b) * 4 + c, at(a, b, c)))
    gx_up = (lax.rem(gx + 1, 8), y, z)
    gx_down = (lax.rem(gx + 7, 8), y, z)
    across = (lax.rem(gx + 7 + 2 * core, 8), y, z)
    bar = pltpu.get_barrier_semaphore()
    near = [along(axis, d) for d in (2, 1, 3) for axis in range(3)] + [across, sister]
    for device in near:
        pl.semaphore_signal(bar, inc=1, device_id=device, device_id_type=MESH)

    def region(n, t, stage, line=0):
        start, rows, order = SHARES[t]
        index = [slice(None) if a in order[:stage] else place[a] for a in range(3)]
        if stage == 2:
            axis = order[1]
            index[axis] = (RX, RY, RZ)[axis][line]
        return gat.at[n].at[index[0], index[1], index[2], pl.ds(start, rows), :]

    def gather_send(n, stage, line=0):
        slot = stage + line
        for t in range(3):
            reg = region(n, t, stage, line)
            for j, d in enumerate((1, 3, 2)):
                send(reg, reg, g_ss.at[n, t, slot, j], g_rs.at[n, t, slot, j], along(SHARES[t][2][stage], d))

    def gather_recv(n, stage, line=0):
        for t in range(3):
            reg = region(n, t, stage, line)
            for j in range(3):
                pltpu.make_async_copy(reg, reg, g_rs.at[n, t, stage + line, j]).wait()

    def gather_one(n):
        gather_send(n, 0)

    def gather_two(n):
        gather_recv(n, 0)
        gather_send(n, 1)
        gather_send(n, 2, 0)

    def gather_three(n):
        gather_recv(n, 1)
        for line in (1, 3, 2):
            gather_send(n, 2, line)

    def gather_done(n):
        for line in (0, 1, 3, 2):
            gather_recv(n, 2, line)

    steps = (
        (gx_up, gx_down),
        ((gx, RY[1], z), (gx, RY[3], z)),
        ((gx, y, RZ[1]), (gx, y, RZ[3])),
    )
    valid = []
    for coordinate, length in ((gx, 8), (y, 4), (z, 4)):
        valid.append(jnp.where(coordinate > 0, 1.0, 0.0).astype(F32))
        valid.append(jnp.where(coordinate < length - 1, 1.0, 0.0).astype(F32))

    def margins(n):
        return (bsend, brecv) if n == 1 else (msend.at[n if n == 0 else n - 1], mrecv.at[n if n == 0 else n - 1])

    def margins_start(n):
        out, into = margins(n)
        for e in range(3):
            up, down = steps[e]
            send(out.at[2 * e + 1], into.at[2 * e], m_ss.at[n, 2 * e], m_rs.at[n, 2 * e], up)
            send(out.at[2 * e], into.at[2 * e + 1], m_ss.at[n, 2 * e + 1], m_rs.at[n, 2 * e + 1], down)

    def margins_wait(n):
        into = margins(n)[1]
        for b in range(6):
            pltpu.make_async_copy(into.at[b], into.at[b], m_rs.at[n, b]).wait()

    def outgoing(n):
        out = margins(n)[0]

        for d in range(0, 6, 2):
            p = dot(emat[d * OVR : (d + 2) * OVR, :], xhl[0:OWN, :])
            q = p[:, 0:NRHS] + p[:, NRHS:]
            out[d] = q[0:OVR]
            out[d + 1] = q[OVR:]

    def import_margins(n):
        margins_wait(n)
        into = margins(n)[1]
        for b in range(6):
            put_pair(xhl, OWN + b * OVR, into[b] * valid[b])

    def product_owned(mat, dst):
        def step(i, carry):
            r = pl.multiple_of(i * 512, 512)
            p = dot(mat[0, pl.ds(r, 512), 0:OWN], xhl[0:OWN, :])
            q = dot(mat[1, pl.ds(r, 512), 0:OWN], xhl[0:OWN, 0:NRHS])
            dst[pl.ds(r, 512), :] = fold(p, q)
            return carry

        lax.fori_loop(0, OWN // 512, step, 0)

    def product_margins(mat, dst):
        def step(i, carry):
            r = pl.multiple_of(i * 512, 512)
            p = dot(mat[0, pl.ds(r, 512), OWN:], xhl[OWN:, :])
            q = dot(mat[1, pl.ds(r, 512), OWN:], xhl[OWN:, 0:NRHS])
            dst[pl.ds(r, 512), :] = dst[pl.ds(r, 512), :] + fold(p, q)
            return carry

        lax.fori_loop(0, OWN // 512, step, 0)

    def solve(n):
        total = jnp.zeros((256, 256), F32)
        for a in range(4):
            for b in range(4):
                put_pair(xg, (a * 4 + b) * 256, gat[n, a, b].reshape(256, NRHS))
            total = total + dot(chl[:, a * 1024 : (a + 1) * 1024], xg[a * 1024 : (a + 1) * 1024, :])
        res = total[0:128, 0:NRHS] + total[0:128, NRHS:] + total[128:256, 0:NRHS]
        psrc[n, 0] = res[0:64]
        psrc[n, 1] = res[64:128]

    def scatter_start(n):
        for c, device in far:
            copy = pltpu.make_async_remote_copy(
                src_ref=psrc.at[n, :, c, :],
                dst_ref=rbuf.at[n, :, chip, :],
                send_sem=s_sem.at[n, 0],
                recv_sem=s_sem.at[n, 1],
                device_id=device,
                device_id_type=MESH,
            )
            copy.start()
        rbuf[n, :, pl.ds(chip, 1), :] = psrc[n, :, pl.ds(chip, 1), :]

    def wait_all(ref, sem):
        pltpu.make_async_copy(ref, ref, sem).wait()

    def swap(n):
        wait_all(rbuf.at[n, :, pl.ds(0, 63), :], s_sem.at[n, 1])
        send(rbuf.at[n], sbuf.at[n], s_sem.at[n, 2], s_sem.at[n, 3], sister).wait_recv()
        first = rbuf[n, 0] + sbuf[n, 1]
        second = rbuf[n, 1] + sbuf[n, 0]
        hi, lo = split(jnp.concatenate([first, second], axis=0))
        p = dot(sel[...], jnp.concatenate([hi, lo], axis=1))
        ssend[n] = (p[:, 0:NRHS] + p[:, NRHS:]).reshape(CHIPS, 8, NRHS)
        for c, device in far:
            copy = pltpu.make_async_remote_copy(
                src_ref=ssend.at[n, c, pl.ds(0, 7)],
                dst_ref=srecv.at[n, chip, pl.ds(0, 7)],
                send_sem=s_sem.at[n, 4],
                recv_sem=s_sem.at[n, 5],
                device_id=device,
                device_id_type=MESH,
            )
            copy.start()
        srecv[n, chip, 0:7] = ssend[n, chip, 0:7]

    def mapped_in(n):
        wait_all(srecv.at[n, pl.ds(0, 63), pl.ds(0, 7)], s_sem.at[n, 5])
        for s in range(7):
            put_pair(mhl, s * K, srecv[n, :, s, :])

    def scatter_drain(n):
        wait_all(rbuf.at[n, :, pl.ds(0, 63), :], s_sem.at[n, 0])
        wait_all(srecv.at[n, pl.ds(0, 63), pl.ds(0, 7)], s_sem.at[n, 4])

    def add_coarse(base, dst):
        mine = mhl[6 * K : 7 * K, :]
        dst[...] = base[...] + fold(dot(bt[0], mine), dot(bt[1], mine[:, 0:NRHS]))

    def apply_coarse(base, dst):
        def step(i, carry):
            r = pl.multiple_of(i * 512, 512)
            p = dot(gmat[0, pl.ds(r, 512), :], mhl[...])
            q = dot(gmat[1, pl.ds(r, 512), :], mhl[:, 0:NRHS])
            dst[pl.ds(r, 512), :] = base[pl.ds(r, 512), :] + fold(p, q)
            return carry

        lax.fori_loop(0, OWN // 512, step, 0)

    def totals_start(n, left, right):
        dsend[n] = jnp.zeros((8, NRHS), F32)
        dsend[n, 0:1, :] = jnp.sum(left[...] * right[...], axis=0, keepdims=True)
        dsend[n, 1:2, :] = jnp.sum(right[...] * right[...], axis=0, keepdims=True)
        return send(dsend.at[n], dsis.at[n], d_sem.at[n, 0], d_sem.at[n, 1], sister)

    def totals_spread(n, copy):
        copy.wait_recv()
        dpair[n] = dsend[n] + dsis[n]
        for c, device in far:
            copy = pltpu.make_async_remote_copy(
                src_ref=dpair.at[n, pl.ds(0, 2)],
                dst_ref=dall.at[n, pl.ds(2 * chip, 2)],
                send_sem=d_sem.at[n, 2],
                recv_sem=d_sem.at[n, 3],
                device_id=device,
                device_id_type=MESH,
            )
            copy.start()
        dall[n, pl.ds(2 * chip, 2)] = dpair[n, 0:2]

    def totals_finish(n):
        wait_all(dall.at[n, pl.ds(0, 126)], d_sem.at[n, 3])
        cross = jnp.sum(dall[n, pl.ds(0, 64, stride=2), :], axis=0, keepdims=True)
        energy = jnp.sum(dall[n, pl.ds(1, 64, stride=2), :], axis=0, keepdims=True)
        wait_all(dall.at[n, pl.ds(0, 126)], d_sem.at[n, 2])
        return cross / energy

    mhl[7 * K :, :] = jnp.zeros((K, 2 * NRHS), BF16)
    loads[0].wait()
    loads[1].wait()
    put_pair(xhl, 0, rv[...])
    hi, lo = split(basis_v[...])
    bhl[0:K, :] = hi
    bhl[K : 2 * K, :] = lo
    gat[0, x, y, z] = stacked(bhl[...], xhl[0:OWN, :])

    def export_rows(g, carry):
        r = pl.multiple_of(g * 16, 16)
        rows = ecol[pl.ds(r, 16), :]
        lanes = lax.broadcasted_iota(jnp.int32, (16, 128), 1)
        one, zero = jnp.ones((16, 128), BF16), jnp.zeros((16, 128), BF16)
        for d in range(6):
            place_d = jnp.broadcast_to(rows[:, d : d + 1], (16, 128)).astype(jnp.int32).astype(jnp.int16)
            for j in range(OWN // 128):
                hit = (lanes + j * 128).astype(jnp.int16) == place_d
                emat[pl.ds(d * OVR + r, 16), j * 128 : (j + 1) * 128] = jnp.where(hit, one, zero)
        return carry

    pltpu.make_async_copy(cinv_v, cinv_v, in_sem.at[7]).wait()
    lane = lax.broadcasted_iota(jnp.int32, (K, 128), 1)

    def column_block(c, kk, half):
        cx, cy, cz = c // 16, lax.rem(c // 4, 4), lax.rem(c, 4)
        j = owner_s[((cx * 2 + kk) * 4 + cy) * 4 + cz]
        pair = lax.shift_right_logical(j, 1)
        tile = cinv_v[pair]
        turned = pltpu.roll(tile, 64, 1)
        same = jnp.full((K, 128), j - 2 * pair, jnp.int32) == half
        return jnp.where(same, tile, turned)

    def column_pair(m, kk):
        return jnp.where(lane < 64, column_block(2 * m, kk, 0), column_block(2 * m + 1, kk, 1))

    def order_other(i, carry):
        for m in range(4):
            m = 4 * i + m
            csend[:, pl.ds(pl.multiple_of(m * 128, 128), 128)] = column_pair(m, 1 - core)
        return carry

    def order_mine(i, carry):
        for m in range(4):
            m = 4 * i + m
            hi, lo = split(column_pair(m, core))
            chl[0:64, pl.ds(pl.multiple_of(m * 128, 128), 128)] = hi
            chl[128:192, pl.ds(pl.multiple_of(m * 128, 128), 128)] = lo
        return carry

    lax.fori_loop(0, 8, order_other, 0)

    def operator_rows(i, carry):
        lanes = lax.broadcasted_iota(jnp.int32, (16, 128), 1)
        row = lax.broadcasted_iota(jnp.int32, (16, 128), 0)
        cell = lanes % 16 == row
        one, zero = jnp.ones((16, 128), BF16), jnp.zeros((16, 128), BF16)
        for g in range(8):
            g = 8 * i + g
            w = jnp.broadcast_to(wrow[pl.ds(g, 1), :], (16, 128))
            t = jnp.broadcast_to(trow[pl.ds(g, 1), :], (16, 128)).astype(jnp.int32)
            high = lax.shift_right_arithmetic(t, 8)
            low = (t - high * 256).astype(F32).astype(BF16)
            whi, wlo = split(jnp.where(cell, w, 0.0))
            tile = jnp.where(cell, high, -1).astype(F32).astype(BF16)
            his, los = [], []
            for j in range(NEXT // 256):
                hit = tile == jnp.asarray(j, BF16)
                his.append(jnp.where(hit, whi, zero))
                los.append(jnp.where(hit, wlo, zero))
            spots = [jnp.where((row + 16 * q).astype(F32).astype(BF16) == low, one, zero) for q in range(16)]
            placed = dot_nt(jnp.concatenate(his + los, axis=0), jnp.concatenate(spots, axis=0)).astype(BF16)
            r = pl.multiple_of(g * 16, 16)
            for j in range(NEXT // 256):
                amat[0, pl.ds(r, 16), j * 256 : (j + 1) * 256] = placed[16 * j : 16 * j + 16]
                amat[1, pl.ds(r, 16), j * 256 : (j + 1) * 256] = placed[160 + 16 * j : 176 + 16 * j]
        return carry

    def build_operator(first, last):
        lax.fori_loop(first, last, operator_rows, 0)

    for i in (3, 4, 5):
        loads[i].wait()
    own_row = lax.broadcasted_iota(jnp.int32, (1, OWN), 1)
    targets = [links_v[k] for k in range(6)]
    weights = [couple_v[k] for k in range(6)]
    centre = diag_v[...] + 6.0
    for k in range(6):
        centre = centre - jnp.where(targets[k] == own_row, weights[k], 0.0)
        gone = targets[k] == own_row
        total = weights[k]
        for m in range(6):
            if m < k:
                gone = gone | (targets[m] == targets[k])
            if m > k:
                total = total + jnp.where(targets[m] == targets[k], weights[m], 0.0)
        tcol[k : k + 1, :] = -total
        ncol[k : k + 1, :] = jnp.where(gone, -1, targets[k]).astype(F32)
    tcol[6:7, :] = centre
    ncol[6:7, :] = own_row.astype(F32)
    tcol[7:8, :] = jnp.zeros((1, OWN), F32)
    ncol[7:8, :] = jnp.full((1, OWN), -1.0, F32)

    def by_groups(ref, into):
        row = lax.broadcasted_iota(jnp.int32, (8, 128), 0)
        part = lax.broadcasted_iota(jnp.int32, (8, 128), 1) // 16
        for c in range(8):
            block = ref[:, c * 128 : (c + 1) * 128]
            turned = jnp.zeros((8, 128), F32)
            for d in range(8):
                moved = block if d == 0 else pltpu.roll(pltpu.roll(block, 8 - d, 0), 16 * d, 1)
                turned = jnp.where((part - row + 8) % 8 == d, moved, turned)
            into[c * 8 : (c + 1) * 8, :] = turned

    by_groups(tcol, wrow)
    by_groups(ncol, trow)

    pl.semaphore_wait(bar, len(near))
    gather_one(0)
    ccopy = send(csend, crecv, c_sem.at[0], c_sem.at[1], sister)
    loads[2].wait()
    tcol[...] = jnp.zeros_like(tcol)
    ncol[...] = jnp.zeros_like(ncol)
    for d in range(6):
        tcol[d : d + 1, 0:OVR] = exports_v[d].astype(F32)
    ecol[...] = tcol[...][:, 0:OVR].T

    lax.fori_loop(0, OVR // 16, export_rows, 0)
    outgoing(0)
    margins_start(0)
    gather_two(0)
    lax.fori_loop(0, 8, order_mine, 0)

    def split_chunk(c):
        load_chunk(c).wait()

        def halves(g, carry):
            r = pl.multiple_of(g * 16, 16)
            hi, lo = split(lstage[c % LSLOTS, pl.ds(r, 16), :])
            linv[0, pl.ds(c * LCH + r, 16), :] = hi
            linv[1, pl.ds(c * LCH + r, 16), :] = lo
            return carry

        lax.fori_loop(0, LCH // 16, halves, 0)
        if c + LSLOTS < NLCH:
            load_chunk(c + LSLOTS).start()

    for c in range(LSLOTS):
        split_chunk(c)
    gather_three(0)
    for c in range(LSLOTS, NLCH):
        split_chunk(c)
    product_owned(linv, l0)
    build_operator(0, A1)
    import_margins(0)
    product_margins(linv, l0)
    put_pair(xhl, 0, l0[...])
    outgoing(2)

    basis_t = basis_v[...].T
    hi, lo = split(basis_t)
    bt[0] = hi
    bt[1] = lo
    bcat[...] = jnp.concatenate([hi, hi, lo, lo], axis=1)
    lane_h = lax.broadcasted_iota(jnp.int32, (128, 128), 1)
    for d in range(0, 6, 2):
        p = dot(emat[d * OVR : (d + 2) * OVR, :], bcat[...])
        q = p[:, 0:NRHS] + p[:, NRHS:]
        bsend[d] = jnp.where(lane_h < 64, q[0:128], q[128:256])
        bsend[d + 1] = jnp.where(lane_h < 64, q[256:384], q[384:512])

    ccopy.wait_recv()

    def sister_rows(m, carry):
        cols = pl.ds(pl.multiple_of(m * 512, 512), 512)
        hi, lo = split(crecv[:, cols])
        chl[64:128, cols] = hi
        chl[192:256, cols] = lo
        return carry

    lax.fori_loop(0, 8, sister_rows, 0)
    build_operator(A1, A2)
    gather_done(0)
    margins_start(2)
    margins_start(1)
    solve(0)
    scatter_start(0)
    build_operator(A2, 8)

    loads[6].wait()
    r_ = lax.broadcasted_iota(jnp.int32, (512, 128), 0)
    q_ = lax.broadcasted_iota(jnp.int32, (512, 128), 1)
    c_, s_ = r_ // 8, r_ % 8
    dx = jnp.where(s_ == 0, 7, jnp.where(s_ == 1, 1, 0))
    dy = jnp.where(s_ == 2, 3, jnp.where(s_ == 3, 1, 0))
    dz = jnp.where(s_ == 4, 3, jnp.where(s_ == 5, 1, 0))
    px = ((c_ // 16) * 2 + core + dx) % 8
    py = ((c_ // 4) % 4 + dy) % 4
    pz = (c_ % 4 + dz) % 4
    wanted = jnp.where(q_ == (px * 4 + py) * 4 + pz, 1.0, 0.0).astype(BF16)
    i_ = lax.broadcasted_iota(jnp.int32, (128, 128), 0)
    ch_ = i_ % 64
    kk_ = (core + i_ // 64) % 2
    block = (((ch_ // 16) * 2 + kk_) * 4 + (ch_ // 4) % 4) * 4 + ch_ % 4
    held = jnp.where(owner_v[...] == block, 1.0, 0.0).astype(BF16)
    sel[...] = dot_nt(wanted, held).astype(BF16)
    swap(0)

    for j in range(0, NEXT, 512):
        p = dot(bhl[...], amat[0, :, j : j + 512])
        hi, lo = split(p[0:K] + p[K:] + dot(bhl[0:K, :], amat[1, :, j : j + 512]))
        bamat[0:K, j : j + 512] = hi
        bamat[K:, j : j + 512] = lo

    margins_wait(1)
    hi, lo = split(jnp.concatenate([basis_t, jnp.zeros_like(basis_t)], axis=1))
    rmat[0:OWN, 0:128] = hi
    rmat[0:OWN, 128:256] = lo
    for b in range(6):
        mask = jnp.where((lane_h < 64) == (b % 2 == 0), valid[b], 0.0)
        top, bottom = brecv[b], pltpu.roll(brecv[b], 64, 1)
        if b % 2 == 1:
            top, bottom = bottom, top
        put_pair(rmat, OWN + b * OVR, top * mask)
        put_pair(rmat, OWN + b * OVR + 128, bottom * mask)
    spans = [(OWN + j * 512, OWN + (j + 1) * 512) for j in range(3)] + [(0, OWN)]
    for j, (start, stop) in enumerate(spans):
        hi, lo = split(stacked(bamat[:, start:stop], rmat[start:stop, :]))
        hmat[0:K, j * 128 : (j + 1) * 128] = hi
        hmat[K:, j * 128 : (j + 1) * 128] = lo
    import_margins(2)
    projected = stacked(bamat[...], xhl[...])
    mapped_in(0)

    gat[1, x, y, z] = projected + stacked(hmat[...], mhl[...])
    gather_one(1)
    add_coarse(l0, u0)
    put_pair(xhl, 0, u0[...])
    into = margins(2)[1]
    for j in range(3):
        start, stop = spans[j]
        part = mhl[j * 128 : (j + 1) * 128, :]
        more = fold(dot(rmat[start:stop, 0:NRHS], part), dot(rmat[start:stop, NRHS:], part[:, 0:NRHS]))
        put_pair(xhl, start, into[2 * j] * valid[2 * j] + more[0:OVR])
        put_pair(xhl, start + OVR, into[2 * j + 1] * valid[2 * j + 1] + more[OVR:])
    product_owned(amat, w0)
    gather_two(1)
    product_margins(amat, w0)
    put_pair(xhl, 0, w0[...])
    outgoing(3)
    gather_three(1)
    margins_start(3)
    dots = totals_start(0, rv, w0)
    product_owned(linv, l1)

    def coarse_columns(i, carry):
        r = pl.multiple_of(i * 512, 512)
        for j, (start, stop) in enumerate(spans):
            p = dot(amat[0, pl.ds(r, 512), start:stop], rmat[start:stop, :])
            q = dot(amat[1, pl.ds(r, 512), start:stop], rmat[start:stop, 0:NRHS])
            hi, lo = split(fold(p, q))
            gmat[0, pl.ds(r, 512), j * 128 : (j + 1) * 128] = hi
            gmat[1, pl.ds(r, 512), j * 128 : (j + 1) * 128] = lo
        return carry

    lax.fori_loop(0, OWN // 512, coarse_columns, 0)
    totals_spread(0, dots)
    gather_done(1)
    solve(1)
    scatter_start(1)
    import_margins(3)
    product_margins(linv, l1)
    put_pair(xhl, 0, l1[...])
    outgoing(4)
    margins_start(4)
    product_owned(amat, al1)
    swap(1)
    alpha0 = totals_finish(0)
    rv[...] = rv[...] - alpha0 * w0[...]
    first = pltpu.make_async_copy(rv, res_ref, out_sem.at[0])
    first.start()
    l0[...] = alpha0 * u0[...]
    second = pltpu.make_async_copy(l0, sol_ref, out_sem.at[1])
    second.start()
    import_margins(4)
    product_margins(amat, al1)
    mapped_in(1)
    apply_coarse(al1, al1)
    w0[...] = w0[...] - alpha0 * al1[...]
    dots = totals_start(1, rv, w0)
    third = pltpu.make_async_copy(w0, image_ref, out_sem.at[2])
    third.start()
    add_coarse(l1, l1)
    l1[...] = u0[...] - alpha0 * l1[...]
    fourth = pltpu.make_async_copy(l1, update_ref, out_sem.at[3])
    totals_spread(1, dots)
    fourth.start()
    alpha_ref[...] = totals_finish(1)

    for copy in pending:
        copy.wait_send()
    scatter_drain(0)
    scatter_drain(1)
    for copy in (first, second, third, fourth):
        copy.wait()


def run(rhs, diagonal, couple, links, exports, linv, basis, cinv, owner):
    field = (OWN, NRHS)
    dma = pltpu.SemaphoreType.DMA
    vm = pltpu.VMEM
    scratch = [
        vm(field, F32),
        vm((K, OWN), F32),
        vm((1, OWN), F32),
        vm((6, 1, OWN), F32),
        vm((6, 1, OWN), jnp.int32),
        vm((6, 1, OVR), jnp.int32),
        vm((1, 128), jnp.int32),
        vm((LSLOTS, LCH, NEXT), F32),
        vm((2, OWN, NEXT), BF16),
        vm((2, OWN, NEXT), BF16),
        vm((6 * OVR, OWN), BF16),
        vm((64, K, 128), F32),
        vm((256, 4096), BF16),
        vm((K, 4096), F32),
        vm((K, 4096), F32),
        vm((2, 4, 4, 4, K, NRHS), F32),
        vm((4096, 256), BF16),
        vm((NEXT, 256), BF16),
        vm((OWN, 256), BF16),
        vm((2, OWN, K), BF16),
        vm((128, OWN), BF16),
        vm((4, 6, OVR, NRHS), F32),
        vm((4, 6, OVR, NRHS), F32),
        vm((6, 128, 128), F32),
        vm((6, 128, 128), F32),
        vm(field, F32),
        vm(field, F32),
        vm(field, F32),
        vm(field, F32),
        vm(field, F32),
        vm((2, OWN, 512), BF16),
        vm((128, 512), BF16),
        vm((512, 128), BF16),
        vm((512, 256), BF16),
        vm((8, OWN), F32),
        vm((8, OWN), F32),
        vm((64, 128), F32),
        vm((64, 128), F32),
        vm((128, NEXT), BF16),
        vm((NEXT, 256), BF16),
        vm((OVR, 8), F32),
        vm((2, 2, CHIPS, NRHS), F32),
        vm((2, 2, CHIPS, NRHS), F32),
        vm((2, 2, CHIPS, NRHS), F32),
        vm((2, CHIPS, 8, NRHS), F32),
        vm((2, CHIPS, 8, NRHS), F32),
        vm((2, 8, NRHS), F32),
        vm((2, 8, NRHS), F32),
        vm((2, 8, NRHS), F32),
        vm((2, 128, NRHS), F32),
        dma((8,)),
        dma((LSLOTS,)),
        dma((2, 3, 6, 3)),
        dma((2, 3, 6, 3)),
        dma((5, 6)),
        dma((5, 6)),
        dma((2,)),
        dma((2, 6)),
        dma((2, 4)),
        dma((4,)),
    ]
    anywhere = pl.BlockSpec(memory_space=pl.ANY)
    return pl.pallas_call(
        kernel,
        out_shape=[jax.ShapeDtypeStruct(field, F32)] * 4 + [jax.ShapeDtypeStruct((1, NRHS), F32)],
        in_specs=[anywhere] * 8 + [pl.BlockSpec(memory_space=pltpu.SMEM), anywhere],
        out_specs=[anywhere] * 4 + [pl.BlockSpec(memory_space=pltpu.VMEM)],
        scratch_shapes=scratch,
        compiler_params=pltpu.CompilerParams(
            collective_id=0, has_side_effects=True, vmem_limit_bytes=63 * 1024 * 1024
        ),
        cost_estimate=pl.CostEstimate(flops=12_000_000_000, bytes_accessed=15_000_000, transcendentals=0),
    )(rhs, diagonal, couple, links, exports, linv, basis, cinv, owner, owner.reshape(1, 128))


def body(rhs, diagonal, couple, neighbours, export_rows, local_inverse, basis, coarse_inverse, owner):
    first, update, residual, image, alpha = run(
        rhs.reshape(OWN, NRHS),
        diagonal.reshape(1, OWN),
        couple.reshape(6, 1, OWN),
        neighbours.reshape(6, 1, OWN),
        export_rows.reshape(6, 1, OVR),
        local_inverse.reshape(OWN, NEXT),
        basis.reshape(K, OWN),
        coarse_inverse,
        owner,
    )
    return (first + alpha * update).reshape(rhs.shape), (residual - alpha * image).reshape(rhs.shape)


def solution(mesh):
    placed = (
        P("gx", "gy", "gz", None, None),
        P("gx", "gy", "gz", None),
        P("gx", "gy", "gz", None, None),
        P("gx", "gy", "gz", None, None),
        P("gx", "gy", "gz", None, None),
        P("gx", "gy", "gz", None, None),
        P("gx", "gy", "gz", None, None),
        P(("gx", "gy", "gz"), None),
        P(),
    )
    return jax.shard_map(
        body,
        mesh=mesh,
        in_specs=placed,
        out_specs=(P("gx", "gy", "gz", None, None), P("gx", "gy", "gz", None, None)),
        check_vma=False,
    )
```

```python
import jax
import jax.numpy as jnp
from jax import lax
from jax.experimental import pallas as pl
from jax.experimental.pallas import tpu as pltpu
from jax.sharding import PartitionSpec as P

F32 = jnp.float32
BF16 = jnp.bfloat16
MESH = pl.DeviceIdType.MESH

OWN = 1024
NRHS = 128
K = 64
OVR = 256
NEXT = 2560
CHIPS = 64
LCH = 128
NLCH = OWN // LCH
LSLOTS = 4

SHARES = ((0, 22, (2, 1, 0)), (22, 21, (0, 2, 1)), (43, 21, (1, 0, 2)))


A1, A2 = 2, 3


def split(x):
    hi = x.astype(BF16)
    lo = (x - hi.astype(F32)).astype(BF16)
    return hi, lo


def put_pair(ref, start, x):
    hi, lo = split(x)
    rows = x.shape[0]
    ref[pl.ds(start, rows), 0:NRHS] = hi
    ref[pl.ds(start, rows), NRHS : 2 * NRHS] = lo


def dot(a, b):
    return jnp.dot(a, b, preferred_element_type=F32)


def dot_nt(a, b):
    return lax.dot_general(a, b, (((1,), (1,)), ((), ())), preferred_element_type=F32)


def fold(p, q):
    return p[:, 0:NRHS] + p[:, NRHS : 2 * NRHS] + q


def stacked(s, x):
    p = dot(s, x)
    half = s.shape[0] // 2
    return fold(p[0:half], p[half:, 0:NRHS])


def ring(v, n):
    return [v] + [lax.rem(v + d, n) for d in range(1, n)]


def hops(d):
    return sum((0, 1, 2, 1)[i] for i in (d // 16, (d // 4) % 4, d % 4))


def kernel(
    rhs_h,
    diag_h,
    couple_h,
    links_h,
    exports_h,
    linv_h,
    basis_h,
    cinv_h,
    owner_s,
    owner_h,
    sol_ref,
    update_ref,
    res_ref,
    image_ref,
    alpha_ref,
    rv,
    basis_v,
    diag_v,
    couple_v,
    links_v,
    exports_v,
    owner_v,
    lstage,
    linv,
    amat,
    emat,
    cinv_v,
    chl,
    csend,
    crecv,
    gat,
    xg,
    xhl,
    bcat,
    bt,
    bhl,
    msend,
    mrecv,
    bsend,
    brecv,
    l0,
    u0,
    w0,
    l1,
    al1,
    gmat,
    hmat,
    sel,
    mhl,
    tcol,
    ncol,
    wrow,
    trow,
    bamat,
    rmat,
    ecol,
    psrc,
    rbuf,
    sbuf,
    ssend,
    srecv,
    dsend,
    dsis,
    dpair,
    dall,
    in_sem,
    l_sem,
    g_ss,
    g_rs,
    m_ss,
    m_rs,
    c_sem,
    s_sem,
    d_sem,
    out_sem,
):
    gx = lax.axis_index("gx")
    y = lax.axis_index("gy")
    z = lax.axis_index("gz")
    x, core = gx // 2, lax.rem(gx, 2)
    chip = (x * 4 + y) * 4 + z
    RX, RY, RZ = ring(x, 4), ring(y, 4), ring(z, 4)
    sister = (x * 2 + 1 - core, y, z)
    place = [x, y, z]

    def at(a, b, c):
        return (a * 2 + core, b, c)

    def along(axis, d):
        p = list(place)
        p[axis] = (RX, RY, RZ)[axis][d]
        return at(*p)

    pending = []

    def send(src, dst, ssem, rsem, device):
        copy = pltpu.make_async_remote_copy(
            src_ref=src, dst_ref=dst, send_sem=ssem, recv_sem=rsem, device_id=device, device_id_type=MESH
        )
        copy.start()
        pending.append(copy)
        return copy

    loads = []
    for i, (src, dst) in enumerate(
        (
            (basis_h, basis_v),
            (rhs_h, rv),
            (exports_h, exports_v),
            (couple_h, couple_v),
            (links_h, links_v),
            (diag_h, diag_v),
            (owner_h, owner_v),
        )
    ):
        copy = pltpu.make_async_copy(src, dst, in_sem.at[i])
        copy.start()
        loads.append(copy)

    def load_columns(t):
        return pltpu.make_async_copy(cinv_h.at[:, pl.ds(pl.multiple_of(t * 128, 128), 128)], cinv_v.at[t], in_sem.at[7])

    def load_column(t, carry):
        load_columns(t).start()
        return carry

    lax.fori_loop(0, 64, load_column, 0)

    def load_chunk(c):
        return pltpu.make_async_copy(linv_h.at[pl.ds(c * LCH, LCH)], lstage.at[c % LSLOTS], l_sem.at[c % LSLOTS])

    for c in range(LSLOTS):
        load_chunk(c).start()

    far = []
    for d in sorted(range(1, CHIPS), key=hops, reverse=True):
        a, b, c = RX[d // 16], RY[(d // 4) % 4], RZ[d % 4]
        far.append(((a * 4 + b) * 4 + c, at(a, b, c)))
    gx_up = (lax.rem(gx + 1, 8), y, z)
    gx_down = (lax.rem(gx + 7, 8), y, z)
    across = (lax.rem(gx + 7 + 2 * core, 8), y, z)
    bar = pltpu.get_barrier_semaphore()
    near = [along(axis, d) for d in (2, 1, 3) for axis in range(3)] + [across, sister]
    for device in near:
        pl.semaphore_signal(bar, inc=1, device_id=device, device_id_type=MESH)

    def region(n, t, stage, line=0):
        start, rows, order = SHARES[t]
        index = [slice(None) if a in order[:stage] else place[a] for a in range(3)]
        if stage == 2:
            axis = order[1]
            index[axis] = (RX, RY, RZ)[axis][line]
        return gat.at[n].at[index[0], index[1], index[2], pl.ds(start, rows), :]

    def gather_send(n, stage, line=0):
        slot = stage + line
        for t in range(3):
            reg = region(n, t, stage, line)
            for j, d in enumerate((1, 3, 2)):
                send(reg, reg, g_ss.at[n, t, slot, j], g_rs.at[n, t, slot, j], along(SHARES[t][2][stage], d))

    def gather_recv(n, stage, line=0):
        for t in range(3):
            reg = region(n, t, stage, line)
            for j in range(3):
                pltpu.make_async_copy(reg, reg, g_rs.at[n, t, stage + line, j]).wait()

    def gather_one(n):
        gather_send(n, 0)

    def gather_two(n):
        gather_recv(n, 0)
        gather_send(n, 1)
        gather_send(n, 2, 0)

    def gather_three(n):
        gather_recv(n, 1)
        for line in (1, 3, 2):
            gather_send(n, 2, line)

    def gather_done(n):
        for line in (0, 1, 3, 2):
            gather_recv(n, 2, line)

    steps = (
        (gx_up, gx_down),
        ((gx, RY[1], z), (gx, RY[3], z)),
        ((gx, y, RZ[1]), (gx, y, RZ[3])),
    )
    valid = []
    for coordinate, length in ((gx, 8), (y, 4), (z, 4)):
        valid.append(jnp.where(coordinate > 0, 1.0, 0.0).astype(F32))
        valid.append(jnp.where(coordinate < length - 1, 1.0, 0.0).astype(F32))

    def margins(n):
        return (bsend, brecv) if n == 1 else (msend.at[n if n == 0 else n - 1], mrecv.at[n if n == 0 else n - 1])

    def margins_start(n):
        out, into = margins(n)
        for e in range(3):
            up, down = steps[e]
            send(out.at[2 * e + 1], into.at[2 * e], m_ss.at[n, 2 * e], m_rs.at[n, 2 * e], up)
            send(out.at[2 * e], into.at[2 * e + 1], m_ss.at[n, 2 * e + 1], m_rs.at[n, 2 * e + 1], down)

    def margins_wait(n):
        into = margins(n)[1]
        for b in range(6):
            pltpu.make_async_copy(into.at[b], into.at[b], m_rs.at[n, b]).wait()

    def outgoing(n):
        out = margins(n)[0]

        for d in range(0, 6, 2):
            p = dot(emat[d * OVR : (d + 2) * OVR, :], xhl[0:OWN, :])
            q = p[:, 0:NRHS] + p[:, NRHS:]
            out[d] = q[0:OVR]
            out[d + 1] = q[OVR:]

    def import_margins(n):
        margins_wait(n)
        into = margins(n)[1]
        for b in range(6):
            put_pair(xhl, OWN + b * OVR, into[b] * valid[b])

    def product_owned(mat, dst):
        def step(i, carry):
            r = pl.multiple_of(i * 512, 512)
            p = dot(mat[0, pl.ds(r, 512), 0:OWN], xhl[0:OWN, :])
            q = dot(mat[1, pl.ds(r, 512), 0:OWN], xhl[0:OWN, 0:NRHS])
            dst[pl.ds(r, 512), :] = fold(p, q)
            return carry

        lax.fori_loop(0, OWN // 512, step, 0)

    def product_margins(mat, dst):
        def step(i, carry):
            r = pl.multiple_of(i * 512, 512)
            p = dot(mat[0, pl.ds(r, 512), OWN:], xhl[OWN:, :])
            q = dot(mat[1, pl.ds(r, 512), OWN:], xhl[OWN:, 0:NRHS])
            dst[pl.ds(r, 512), :] = dst[pl.ds(r, 512), :] + fold(p, q)
            return carry

        lax.fori_loop(0, OWN // 512, step, 0)

    def solve(n):
        total = jnp.zeros((256, 256), F32)
        for a in range(4):
            for b in range(4):
                put_pair(xg, (a * 4 + b) * 256, gat[n, a, b].reshape(256, NRHS))
            total = total + dot(chl[:, a * 1024 : (a + 1) * 1024], xg[a * 1024 : (a + 1) * 1024, :])
        res = total[0:128, 0:NRHS] + total[0:128, NRHS:] + total[128:256, 0:NRHS]
        psrc[n, 0] = res[0:64]
        psrc[n, 1] = res[64:128]

    def scatter_start(n):
        for c, device in far:
            copy = pltpu.make_async_remote_copy(
                src_ref=psrc.at[n, :, c, :],
                dst_ref=rbuf.at[n, :, chip, :],
                send_sem=s_sem.at[n, 0],
                recv_sem=s_sem.at[n, 1],
                device_id=device,
                device_id_type=MESH,
            )
            copy.start()
        rbuf[n, :, pl.ds(chip, 1), :] = psrc[n, :, pl.ds(chip, 1), :]

    def wait_all(ref, sem):
        pltpu.make_async_copy(ref, ref, sem).wait()

    def swap(n):
        wait_all(rbuf.at[n, :, pl.ds(0, 63), :], s_sem.at[n, 1])
        send(rbuf.at[n], sbuf.at[n], s_sem.at[n, 2], s_sem.at[n, 3], sister).wait_recv()
        first = rbuf[n, 0] + sbuf[n, 1]
        second = rbuf[n, 1] + sbuf[n, 0]
        hi, lo = split(jnp.concatenate([first, second], axis=0))
        p = dot(sel[...], jnp.concatenate([hi, lo], axis=1))
        ssend[n] = (p[:, 0:NRHS] + p[:, NRHS:]).reshape(CHIPS, 8, NRHS)
        for c, device in far:
            copy = pltpu.make_async_remote_copy(
                src_ref=ssend.at[n, c, pl.ds(0, 7)],
                dst_ref=srecv.at[n, chip, pl.ds(0, 7)],
                send_sem=s_sem.at[n, 4],
                recv_sem=s_sem.at[n, 5],
                device_id=device,
                device_id_type=MESH,
            )
            copy.start()
        srecv[n, chip, 0:7] = ssend[n, chip, 0:7]

    def mapped_in(n):
        wait_all(srecv.at[n, pl.ds(0, 63), pl.ds(0, 7)], s_sem.at[n, 5])
        for s in range(7):
            put_pair(mhl, s * K, srecv[n, :, s, :])

    def scatter_drain(n):
        wait_all(rbuf.at[n, :, pl.ds(0, 63), :], s_sem.at[n, 0])
        wait_all(srecv.at[n, pl.ds(0, 63), pl.ds(0, 7)], s_sem.at[n, 4])

    def add_coarse(base, dst):
        mine = mhl[6 * K : 7 * K, :]
        dst[...] = base[...] + fold(dot(bt[0], mine), dot(bt[1], mine[:, 0:NRHS]))

    def apply_coarse(base, dst):
        def step(i, carry):
            r = pl.multiple_of(i * 512, 512)
            p = dot(gmat[0, pl.ds(r, 512), :], mhl[...])
            q = dot(gmat[1, pl.ds(r, 512), :], mhl[:, 0:NRHS])
            dst[pl.ds(r, 512), :] = base[pl.ds(r, 512), :] + fold(p, q)
            return carry

        lax.fori_loop(0, OWN // 512, step, 0)

    def totals_start(n, left, right):
        dsend[n] = jnp.zeros((8, NRHS), F32)
        dsend[n, 0:1, :] = jnp.sum(left[...] * right[...], axis=0, keepdims=True)
        dsend[n, 1:2, :] = jnp.sum(right[...] * right[...], axis=0, keepdims=True)
        return send(dsend.at[n], dsis.at[n], d_sem.at[n, 0], d_sem.at[n, 1], sister)

    def totals_spread(n, copy):
        copy.wait_recv()
        dpair[n] = dsend[n] + dsis[n]
        for c, device in far:
            copy = pltpu.make_async_remote_copy(
                src_ref=dpair.at[n, pl.ds(0, 2)],
                dst_ref=dall.at[n, pl.ds(2 * chip, 2)],
                send_sem=d_sem.at[n, 2],
                recv_sem=d_sem.at[n, 3],
                device_id=device,
                device_id_type=MESH,
            )
            copy.start()
        dall[n, pl.ds(2 * chip, 2)] = dpair[n, 0:2]

    def totals_finish(n):
        wait_all(dall.at[n, pl.ds(0, 126)], d_sem.at[n, 3])
        cross = jnp.sum(dall[n, pl.ds(0, 64, stride=2), :], axis=0, keepdims=True)
        energy = jnp.sum(dall[n, pl.ds(1, 64, stride=2), :], axis=0, keepdims=True)
        wait_all(dall.at[n, pl.ds(0, 126)], d_sem.at[n, 2])
        return cross / energy

    mhl[7 * K :, :] = jnp.zeros((K, 2 * NRHS), BF16)
    loads[0].wait()
    loads[1].wait()
    put_pair(xhl, 0, rv[...])
    hi, lo = split(basis_v[...])
    bhl[0:K, :] = hi
    bhl[K : 2 * K, :] = lo
    gat[0, x, y, z] = stacked(bhl[...], xhl[0:OWN, :])

    def export_rows(g, carry):
        r = pl.multiple_of(g * 16, 16)
        rows = ecol[pl.ds(r, 16), :]
        lanes = lax.broadcasted_iota(jnp.int32, (16, 128), 1)
        one, zero = jnp.ones((16, 128), BF16), jnp.zeros((16, 128), BF16)
        for d in range(6):
            place_d = jnp.broadcast_to(rows[:, d : d + 1], (16, 128)).astype(jnp.int32).astype(jnp.int16)
            for j in range(OWN // 128):
                hit = (lanes + j * 128).astype(jnp.int16) == place_d
                emat[pl.ds(d * OVR + r, 16), j * 128 : (j + 1) * 128] = jnp.where(hit, one, zero)
        return carry

    pltpu.make_async_copy(cinv_v, cinv_v, in_sem.at[7]).wait()
    lane = lax.broadcasted_iota(jnp.int32, (K, 128), 1)

    def column_block(c, kk, half):
        cx, cy, cz = c // 16, lax.rem(c // 4, 4), lax.rem(c, 4)
        j = owner_s[((cx * 2 + kk) * 4 + cy) * 4 + cz]
        pair = lax.shift_right_logical(j, 1)
        tile = cinv_v[pair]
        turned = pltpu.roll(tile, 64, 1)
        same = jnp.full((K, 128), j - 2 * pair, jnp.int32) == half
        return jnp.where(same, tile, turned)

    def column_pair(m, kk):
        return jnp.where(lane < 64, column_block(2 * m, kk, 0), column_block(2 * m + 1, kk, 1))

    def order_other(i, carry):
        for m in range(4):
            m = 4 * i + m
            csend[:, pl.ds(pl.multiple_of(m * 128, 128), 128)] = column_pair(m, 1 - core)
        return carry

    def order_mine(i, carry):
        for m in range(4):
            m = 4 * i + m
            hi, lo = split(column_pair(m, core))
            chl[0:64, pl.ds(pl.multiple_of(m * 128, 128), 128)] = hi
            chl[128:192, pl.ds(pl.multiple_of(m * 128, 128), 128)] = lo
        return carry

    lax.fori_loop(0, 8, order_other, 0)

    def operator_rows(i, carry):
        lanes = lax.broadcasted_iota(jnp.int32, (16, 128), 1)
        row = lax.broadcasted_iota(jnp.int32, (16, 128), 0)
        cell = lanes % 16 == row
        one, zero = jnp.ones((16, 128), BF16), jnp.zeros((16, 128), BF16)
        for g in range(8):
            g = 8 * i + g
            w = jnp.broadcast_to(wrow[pl.ds(g, 1), :], (16, 128))
            t = jnp.broadcast_to(trow[pl.ds(g, 1), :], (16, 128)).astype(jnp.int32)
            high = lax.shift_right_arithmetic(t, 8)
            low = (t - high * 256).astype(F32).astype(BF16)
            whi, wlo = split(jnp.where(cell, w, 0.0))
            tile = jnp.where(cell, high, -1).astype(F32).astype(BF16)
            his, los = [], []
            for j in range(NEXT // 256):
                hit = tile == jnp.asarray(j, BF16)
                his.append(jnp.where(hit, whi, zero))
                los.append(jnp.where(hit, wlo, zero))
            spots = [jnp.where((row + 16 * q).astype(F32).astype(BF16) == low, one, zero) for q in range(16)]
            placed = dot_nt(jnp.concatenate(his + los, axis=0), jnp.concatenate(spots, axis=0)).astype(BF16)
            r = pl.multiple_of(g * 16, 16)
            for j in range(NEXT // 256):
                amat[0, pl.ds(r, 16), j * 256 : (j + 1) * 256] = placed[16 * j : 16 * j + 16]
                amat[1, pl.ds(r, 16), j * 256 : (j + 1) * 256] = placed[160 + 16 * j : 176 + 16 * j]
        return carry

    def build_operator(first, last):
        lax.fori_loop(first, last, operator_rows, 0)

    for i in (3, 4, 5):
        loads[i].wait()
    own_row = lax.broadcasted_iota(jnp.int32, (1, OWN), 1)
    targets = [links_v[k] for k in range(6)]
    weights = [couple_v[k] for k in range(6)]
    centre = diag_v[...] + 6.0
    for k in range(6):
        centre = centre - jnp.where(targets[k] == own_row, weights[k], 0.0)
        gone = targets[k] == own_row
        total = weights[k]
        for m in range(6):
            if m < k:
                gone = gone | (targets[m] == targets[k])
            if m > k:
                total = total + jnp.where(targets[m] == targets[k], weights[m], 0.0)
        tcol[k : k + 1, :] = -total
        ncol[k : k + 1, :] = jnp.where(gone, -1, targets[k]).astype(F32)
    tcol[6:7, :] = centre
    ncol[6:7, :] = own_row.astype(F32)
    tcol[7:8, :] = jnp.zeros((1, OWN), F32)
    ncol[7:8, :] = jnp.full((1, OWN), -1.0, F32)

    def by_groups(ref, into):
        row = lax.broadcasted_iota(jnp.int32, (8, 128), 0)
        part = lax.broadcasted_iota(jnp.int32, (8, 128), 1) // 16
        for c in range(8):
            block = ref[:, c * 128 : (c + 1) * 128]
            turned = jnp.zeros((8, 128), F32)
            for d in range(8):
                moved = block if d == 0 else pltpu.roll(pltpu.roll(block, 8 - d, 0), 16 * d, 1)
                turned = jnp.where((part - row + 8) % 8 == d, moved, turned)
            into[c * 8 : (c + 1) * 8, :] = turned

    by_groups(tcol, wrow)
    by_groups(ncol, trow)

    pl.semaphore_wait(bar, len(near))
    gather_one(0)
    ccopy = send(csend, crecv, c_sem.at[0], c_sem.at[1], sister)
    loads[2].wait()
    tcol[...] = jnp.zeros_like(tcol)
    ncol[...] = jnp.zeros_like(ncol)
    for d in range(6):
        tcol[d : d + 1, 0:OVR] = exports_v[d].astype(F32)
    ecol[...] = tcol[...][:, 0:OVR].T

    lax.fori_loop(0, OVR // 16, export_rows, 0)
    outgoing(0)
    gather_two(0)
    margins_start(0)
    lax.fori_loop(0, 8, order_mine, 0)

    def split_chunk(c):
        load_chunk(c).wait()

        def halves(g, carry):
            r = pl.multiple_of(g * 16, 16)
            hi, lo = split(lstage[c % LSLOTS, pl.ds(r, 16), :])
            linv[0, pl.ds(c * LCH + r, 16), :] = hi
            linv[1, pl.ds(c * LCH + r, 16), :] = lo
            return carry

        lax.fori_loop(0, LCH // 16, halves, 0)
        if c + LSLOTS < NLCH:
            load_chunk(c + LSLOTS).start()

    for c in range(LSLOTS):
        split_chunk(c)
    gather_three(0)
    for c in range(LSLOTS, NLCH):
        split_chunk(c)
    product_owned(linv, l0)
    build_operator(0, A1)
    import_margins(0)
    product_margins(linv, l0)
    put_pair(xhl, 0, l0[...])
    outgoing(2)

    basis_t = basis_v[...].T
    hi, lo = split(basis_t)
    bt[0] = hi
    bt[1] = lo
    bcat[...] = jnp.concatenate([hi, hi, lo, lo], axis=1)
    lane_h = lax.broadcasted_iota(jnp.int32, (128, 128), 1)
    for d in range(0, 6, 2):
        p = dot(emat[d * OVR : (d + 2) * OVR, :], bcat[...])
        q = p[:, 0:NRHS] + p[:, NRHS:]
        bsend[d] = jnp.where(lane_h < 64, q[0:128], q[128:256])
        bsend[d + 1] = jnp.where(lane_h < 64, q[256:384], q[384:512])

    ccopy.wait_recv()

    def sister_rows(m, carry):
        cols = pl.ds(pl.multiple_of(m * 512, 512), 512)
        hi, lo = split(crecv[:, cols])
        chl[64:128, cols] = hi
        chl[192:256, cols] = lo
        return carry

    lax.fori_loop(0, 8, sister_rows, 0)
    build_operator(A1, A2)
    gather_done(0)
    solve(0)
    scatter_start(0)
    margins_start(1)
    margins_start(2)
    build_operator(A2, 8)

    loads[6].wait()
    r_ = lax.broadcasted_iota(jnp.int32, (512, 128), 0)
    q_ = lax.broadcasted_iota(jnp.int32, (512, 128), 1)
    c_, s_ = r_ // 8, r_ % 8
    dx = jnp.where(s_ == 0, 7, jnp.where(s_ == 1, 1, 0))
    dy = jnp.where(s_ == 2, 3, jnp.where(s_ == 3, 1, 0))
    dz = jnp.where(s_ == 4, 3, jnp.where(s_ == 5, 1, 0))
    px = ((c_ // 16) * 2 + core + dx) % 8
    py = ((c_ // 4) % 4 + dy) % 4
    pz = (c_ % 4 + dz) % 4
    wanted = jnp.where(q_ == (px * 4 + py) * 4 + pz, 1.0, 0.0).astype(BF16)
    i_ = lax.broadcasted_iota(jnp.int32, (128, 128), 0)
    ch_ = i_ % 64
    kk_ = (core + i_ // 64) % 2
    block = (((ch_ // 16) * 2 + kk_) * 4 + (ch_ // 4) % 4) * 4 + ch_ % 4
    held = jnp.where(owner_v[...] == block, 1.0, 0.0).astype(BF16)
    sel[...] = dot_nt(wanted, held).astype(BF16)
    swap(0)

    for j in range(0, NEXT, 512):
        p = dot(bhl[...], amat[0, :, j : j + 512])
        hi, lo = split(p[0:K] + p[K:] + dot(bhl[0:K, :], amat[1, :, j : j + 512]))
        bamat[0:K, j : j + 512] = hi
        bamat[K:, j : j + 512] = lo

    margins_wait(1)
    hi, lo = split(jnp.concatenate([basis_t, jnp.zeros_like(basis_t)], axis=1))
    rmat[0:OWN, 0:128] = hi
    rmat[0:OWN, 128:256] = lo
    for b in range(6):
        mask = jnp.where((lane_h < 64) == (b % 2 == 0), valid[b], 0.0)
        top, bottom = brecv[b], pltpu.roll(brecv[b], 64, 1)
        if b % 2 == 1:
            top, bottom = bottom, top
        put_pair(rmat, OWN + b * OVR, top * mask)
        put_pair(rmat, OWN + b * OVR + 128, bottom * mask)
    spans = [(OWN + j * 512, OWN + (j + 1) * 512) for j in range(3)] + [(0, OWN)]
    for j, (start, stop) in enumerate(spans):
        hi, lo = split(stacked(bamat[:, start:stop], rmat[start:stop, :]))
        hmat[0:K, j * 128 : (j + 1) * 128] = hi
        hmat[K:, j * 128 : (j + 1) * 128] = lo
    import_margins(2)
    projected = stacked(bamat[...], xhl[...])
    mapped_in(0)

    gat[1, x, y, z] = projected + stacked(hmat[...], mhl[...])
    gather_one(1)
    add_coarse(l0, u0)
    put_pair(xhl, 0, u0[...])
    into = margins(2)[1]
    for j in range(3):
        start, stop = spans[j]
        part = mhl[j * 128 : (j + 1) * 128, :]
        more = fold(dot(rmat[start:stop, 0:NRHS], part), dot(rmat[start:stop, NRHS:], part[:, 0:NRHS]))
        put_pair(xhl, start, into[2 * j] * valid[2 * j] + more[0:OVR])
        put_pair(xhl, start + OVR, into[2 * j + 1] * valid[2 * j + 1] + more[OVR:])
    product_owned(amat, w0)
    gather_two(1)
    product_margins(amat, w0)
    put_pair(xhl, 0, w0[...])
    outgoing(3)
    gather_three(1)
    margins_start(3)
    dots = totals_start(0, rv, w0)
    product_owned(linv, l1)

    def coarse_columns(i, carry):
        r = pl.multiple_of(i * 512, 512)
        for j, (start, stop) in enumerate(spans):
            p = dot(amat[0, pl.ds(r, 512), start:stop], rmat[start:stop, :])
            q = dot(amat[1, pl.ds(r, 512), start:stop], rmat[start:stop, 0:NRHS])
            hi, lo = split(fold(p, q))
            gmat[0, pl.ds(r, 512), j * 128 : (j + 1) * 128] = hi
            gmat[1, pl.ds(r, 512), j * 128 : (j + 1) * 128] = lo
        return carry

    lax.fori_loop(0, OWN // 512, coarse_columns, 0)
    totals_spread(0, dots)
    gather_done(1)
    solve(1)
    scatter_start(1)
    import_margins(3)
    product_margins(linv, l1)
    put_pair(xhl, 0, l1[...])
    outgoing(4)
    margins_start(4)
    product_owned(amat, al1)
    swap(1)
    alpha0 = totals_finish(0)
    rv[...] = rv[...] - alpha0 * w0[...]
    first = pltpu.make_async_copy(rv, res_ref, out_sem.at[0])
    first.start()
    l0[...] = alpha0 * u0[...]
    second = pltpu.make_async_copy(l0, sol_ref, out_sem.at[1])
    second.start()
    import_margins(4)
    product_margins(amat, al1)
    mapped_in(1)
    apply_coarse(al1, al1)
    w0[...] = w0[...] - alpha0 * al1[...]
    dots = totals_start(1, rv, w0)
    third = pltpu.make_async_copy(w0, image_ref, out_sem.at[2])
    third.start()
    add_coarse(l1, l1)
    l1[...] = u0[...] - alpha0 * l1[...]
    fourth = pltpu.make_async_copy(l1, update_ref, out_sem.at[3])
    totals_spread(1, dots)
    fourth.start()
    alpha_ref[...] = totals_finish(1)

    for copy in pending:
        copy.wait_send()
    scatter_drain(0)
    scatter_drain(1)
    for copy in (first, second, third, fourth):
        copy.wait()


def run(rhs, diagonal, couple, links, exports, linv, basis, cinv, owner):
    field = (OWN, NRHS)
    dma = pltpu.SemaphoreType.DMA
    vm = pltpu.VMEM
    scratch = [
        vm(field, F32),
        vm((K, OWN), F32),
        vm((1, OWN), F32),
        vm((6, 1, OWN), F32),
        vm((6, 1, OWN), jnp.int32),
        vm((6, 1, OVR), jnp.int32),
        vm((1, 128), jnp.int32),
        vm((LSLOTS, LCH, NEXT), F32),
        vm((2, OWN, NEXT), BF16),
        vm((2, OWN, NEXT), BF16),
        vm((6 * OVR, OWN), BF16),
        vm((64, K, 128), F32),
        vm((256, 4096), BF16),
        vm((K, 4096), F32),
        vm((K, 4096), F32),
        vm((2, 4, 4, 4, K, NRHS), F32),
        vm((4096, 256), BF16),
        vm((NEXT, 256), BF16),
        vm((OWN, 256), BF16),
        vm((2, OWN, K), BF16),
        vm((128, OWN), BF16),
        vm((4, 6, OVR, NRHS), F32),
        vm((4, 6, OVR, NRHS), F32),
        vm((6, 128, 128), F32),
        vm((6, 128, 128), F32),
        vm(field, F32),
        vm(field, F32),
        vm(field, F32),
        vm(field, F32),
        vm(field, F32),
        vm((2, OWN, 512), BF16),
        vm((128, 512), BF16),
        vm((512, 128), BF16),
        vm((512, 256), BF16),
        vm((8, OWN), F32),
        vm((8, OWN), F32),
        vm((64, 128), F32),
        vm((64, 128), F32),
        vm((128, NEXT), BF16),
        vm((NEXT, 256), BF16),
        vm((OVR, 8), F32),
        vm((2, 2, CHIPS, NRHS), F32),
        vm((2, 2, CHIPS, NRHS), F32),
        vm((2, 2, CHIPS, NRHS), F32),
        vm((2, CHIPS, 8, NRHS), F32),
        vm((2, CHIPS, 8, NRHS), F32),
        vm((2, 8, NRHS), F32),
        vm((2, 8, NRHS), F32),
        vm((2, 8, NRHS), F32),
        vm((2, 128, NRHS), F32),
        dma((8,)),
        dma((LSLOTS,)),
        dma((2, 3, 6, 3)),
        dma((2, 3, 6, 3)),
        dma((5, 6)),
        dma((5, 6)),
        dma((2,)),
        dma((2, 6)),
        dma((2, 4)),
        dma((4,)),
    ]
    anywhere = pl.BlockSpec(memory_space=pl.ANY)
    return pl.pallas_call(
        kernel,
        out_shape=[jax.ShapeDtypeStruct(field, F32)] * 4 + [jax.ShapeDtypeStruct((1, NRHS), F32)],
        in_specs=[anywhere] * 8 + [pl.BlockSpec(memory_space=pltpu.SMEM), anywhere],
        out_specs=[anywhere] * 4 + [pl.BlockSpec(memory_space=pltpu.VMEM)],
        scratch_shapes=scratch,
        compiler_params=pltpu.CompilerParams(
            collective_id=0, has_side_effects=True, vmem_limit_bytes=63 * 1024 * 1024
        ),
        cost_estimate=pl.CostEstimate(flops=12_000_000_000, bytes_accessed=15_000_000, transcendentals=0),
    )(rhs, diagonal, couple, links, exports, linv, basis, cinv, owner, owner.reshape(1, 128))


def body(rhs, diagonal, couple, neighbours, export_rows, local_inverse, basis, coarse_inverse, owner):
    first, update, residual, image, alpha = run(
        rhs.reshape(OWN, NRHS),
        diagonal.reshape(1, OWN),
        couple.reshape(6, 1, OWN),
        neighbours.reshape(6, 1, OWN),
        export_rows.reshape(6, 1, OVR),
        local_inverse.reshape(OWN, NEXT),
        basis.reshape(K, OWN),
        coarse_inverse,
        owner,
    )
    return (first + alpha * update).reshape(rhs.shape), (residual - alpha * image).reshape(rhs.shape)


def solution(mesh):
    placed = (
        P("gx", "gy", "gz", None, None),
        P("gx", "gy", "gz", None),
        P("gx", "gy", "gz", None, None),
        P("gx", "gy", "gz", None, None),
        P("gx", "gy", "gz", None, None),
        P("gx", "gy", "gz", None, None),
        P("gx", "gy", "gz", None, None),
        P(("gx", "gy", "gz"), None),
        P(),
    )
    return jax.shard_map(
        body,
        mesh=mesh,
        in_specs=placed,
        out_specs=(P("gx", "gy", "gz", None, None), P("gx", "gy", "gz", None, None)),
        check_vma=False,
    )
```
